256 devices in a mesh: member: 64 (over z, y, x_lo), tile: 4 (over x_hi, core).
Axes of the slice: x: 4 (x_hi: 2, x_lo: 2; x = x_hi * 2 + x_lo), y: 4, z: 8, core: 2. Of those that a mesh axis runs over, the one named last changes fastest.
Arguments:
- features: bfloat16 [64, 128, 32, 2048], P('member', None, 'tile')
- residual_state: float32 [64, 4, 32, 2048], P('member', None, 'tile'), may hold values from -6 to 6
- noise: float32 [64, 4, 32, 2048], P('member', None, 'tile'), may hold values from -6 to 6
- regression_mean: float32 [4, 32, 2048], P(None, 'tile', 'member'), may hold values from -6 to 6
- step_index: int32 [1], replicated, may hold values from 9 to 16
- conv_first: bfloat16 [9, 128, 128], replicated, may hold values from -0.1875 to 0.1875
- conv_second: bfloat16 [9, 128, 128], replicated, may hold values from -0.1875 to 0.1875
- head_weight: bfloat16 [4, 128], replicated, may hold values from -0.5 to 0.5
- spread_target: float32 [4], replicated, may hold values from 0.5 to 4
Outputs:
- ensemble_field: float32 [64, 4, 32, 2048], P('member', None, 'tile')
- next_state: float32 [64, 4, 32, 2048], P('member', None, 'tile')
The draws below stay inside these ranges and needn't reach their ends.
All inputs are finite; a program needn't handle non-finite values.
Results may differ from the reference program's by a relative error of at most 0.0013.
Values may be sent and summed in bfloat16 or wider, within the bound.
No kernel may reach another device: no remote copies, remote signals or barrier semaphores. Data moves between devices by JAX's collectives and lax.ppermute only.
A program may use at most 128 MiB of HBM per device.

```python
import math
import jax
import jax.numpy as jnp
from jax import lax

CHANNELS = 128
GROUPS = 32
OUTPUTS = 4
COLS = 2048
ROWS = 32
MEMBERS = 64


def draw_features(key, part):
    key = jax.random.fold_in(key, 7)
    key_values, key_rows, key_cols = jax.random.split(key, 3)
    shape = (MEMBERS, CHANNELS, ROWS, COLS)
    position = jnp.arange(ROWS).astype(jnp.float32) / max(ROWS - 1, 1)
    ramp = jnp.exp(position * math.log(3.0))
    row_scale = ramp * jnp.exp(jax.random.uniform(key_rows, (ROWS,), jnp.float32, 0.0, math.log(3.3)))
    col_scale = jnp.exp(jax.random.uniform(key_cols, (COLS,), jnp.float32, 0.0, math.log(3.3)))
    scale = row_scale[:, None] * col_scale[None, :] / 6.0
    values = jax.random.normal(key_values, shape, jnp.float32)
    return (values * scale[None, None]).astype(jnp.bfloat16)


def level_of(rng, extent, cuts, low, top_value):
    factor_of = 1.0
    for dim, blocks in cuts:
        steps = jax.random.uniform(jax.random.fold_in(jax.random.fold_in(rng, 6), dim), (blocks,), jnp.float32, low / len(cuts), top_value / len(cuts))
        factor_of = factor_of * jnp.repeat(jnp.exp(steps), extent[dim] // blocks).reshape((-1,) + (1,) * (len(extent) - 1 - dim))
    return factor_of


def normal_values(own_key, shape, scale, bound, cuts=(), held_as=jnp.bfloat16):
    result = jax.random.normal(own_key, shape, jnp.float32) * scale
    if len(cuts) > 0:
        result = level_of(own_key, shape, cuts, -0.22, 0.18) * result
    return jnp.clip(result, min=-bound, max=bound).astype(held_as)


def setup_inputs(seed: int = 0) -> dict:
    arg_keys = jax.random.split(jax.random.key(seed), 10)
    return {
        "features": draw_features(jax.random.fold_in(arg_keys[9], 71), 0),
        "residual_state": normal_values(arg_keys[1], (MEMBERS, OUTPUTS, ROWS, COLS), 1.0, 6.0, ((0, 64), (2, 4)), jnp.float32),
        "noise": normal_values(arg_keys[2], (MEMBERS, OUTPUTS, ROWS, COLS), 1.0, 6.0, ((0, 64), (2, 4)), jnp.float32),
        "regression_mean": normal_values(arg_keys[3], (OUTPUTS, ROWS, COLS), 1.0, 6.0, ((1, 4), (2, 64)), jnp.float32),
        "step_index": jax.random.randint(arg_keys[4], (1,), 9, 17).astype(jnp.int32),
        "conv_first": normal_values(arg_keys[5], (9, CHANNELS, CHANNELS), (9 * CHANNELS) ** -0.5, 0.1875),
        "conv_second": normal_values(arg_keys[6], (9, CHANNELS, CHANNELS), (9 * CHANNELS) ** -0.5, 0.1875),
        "head_weight": normal_values(arg_keys[7], (OUTPUTS, CHANNELS), CHANNELS ** -0.5, 0.5),
        "spread_target": jnp.clip(jnp.exp(jax.random.uniform(arg_keys[8], (OUTPUTS,), jnp.float32, math.log(0.5), math.log(4.0))), 0.5, 4.0),
    }


def plan(step_index):
    steps = jnp.arange(18).astype(jnp.float32)
    upper = 800.0 ** (1.0 / 7.0)
    lower = 0.002 ** (1.0 / 7.0)
    sigmas = (upper + steps / 17.0 * (lower - upper)) ** 7
    places = jnp.arange(18).astype(jnp.int32)
    sigma = jnp.sum(jnp.where(places == step_index[0], sigmas, 0.0))
    sigma_next = jnp.sum(jnp.where(places == step_index[0] + 1, sigmas, 0.0))
    return (sigma, sigma_next)

def group_norm(block):
    values = block.astype(jnp.float32).reshape(GROUPS, -1, block.shape[1], block.shape[2])
    mean = lax.optimization_barrier(jnp.mean(values, axis=(1, 2, 3), keepdims=True))
    centred = values - mean
    var = lax.optimization_barrier(jnp.mean(centred * centred, axis=(1, 2, 3), keepdims=True))
    normed = centred * lax.rsqrt(var + 1e-05)
    return jax.nn.silu(normed).astype(jnp.bfloat16).reshape(block.shape)

def convolve(activ, kernel):
    height, width = (activ.shape[1], activ.shape[2])
    padded = jnp.pad(activ.astype(jnp.float32), ((0, 0), (1, 1), (1, 1)))
    total = jnp.zeros((kernel.shape[1], height, width), jnp.float32)
    for row_tap in range(3):
        for col_tap in range(3):
            weight = kernel[3 * row_tap + col_tap].astype(jnp.float32)
            window = padded[:, row_tap:row_tap + height, col_tap:col_tap + width]
            total = total + jnp.einsum('oc,chw->ohw', weight, window)
    return total

def reference(features, residual_state, noise, regression_mean, step_index, conv_first, conv_second, head_weight, spread_target):
    sigma, sigma_next = plan(step_index)
    sigma_hat = 1.25 * sigma

    def network_of(member_features):
        activ_first = group_norm(member_features)
        hidden_first = convolve(activ_first, conv_first).astype(jnp.bfloat16)
        activ_second = group_norm(hidden_first)
        block_out = (member_features.astype(jnp.float32) + convolve(activ_second, conv_second)).astype(jnp.bfloat16)
        return jnp.einsum('oc,chw->ohw', head_weight.astype(jnp.float32), block_out.astype(jnp.float32))
    network = lax.map(network_of, features)
    state_hat = residual_state + jnp.sqrt(sigma_hat * sigma_hat - sigma * sigma) * noise
    c_skip = 0.25 / (sigma_hat * sigma_hat + 0.25)
    c_out = 0.5 * sigma_hat / jnp.sqrt(sigma_hat * sigma_hat + 0.25)
    denoised = c_skip * state_hat + c_out * network
    next_state = state_hat + (sigma_next - sigma_hat) / sigma_hat * (state_hat - denoised)
    ens_mean = lax.optimization_barrier(jnp.mean(next_state, axis=0))
    ens_var = lax.optimization_barrier(jnp.mean(next_state * next_state, axis=0)) - ens_mean * ens_mean
    factor = jnp.sqrt(1.0 + spread_target[:, None, None] / (ens_var + 1.0))
    ensemble_field = regression_mean[None] + ens_mean[None] + (next_state - ens_mean[None]) * factor[None]
    return (ensemble_field, next_state)
```

```python
import functools

import jax
import jax.numpy as jnp
from jax import lax
from jax.experimental import pallas as pl
from jax.experimental.pallas import tpu as pltpu
from jax.sharding import PartitionSpec as P

GROUP = 4
TILES = 4
F32, BF16 = jnp.float32, jnp.bfloat16
VM = pl.BlockSpec(memory_space=pltpu.VMEM)
SM = pl.BlockSpec(memory_space=pltpu.SMEM)
PARAMS = pltpu.CompilerParams(vmem_limit_bytes=56 * 1024 * 1024)


def group_total(row):
    lane = lax.broadcasted_iota(jnp.int32, row.shape, 1)
    size = row.shape[1]
    for step in (1, 2):
        up = pltpu.roll(row, step, 1)
        down = pltpu.roll(row, size - step, 1)
        row = row + jnp.where((lane & step) == 0, down, up)
    return row


def merged(parts, count):
    means = [p[0:1, :] for p in parts]
    devs = [p[1:2, :] for p in parts]
    members = len(parts) * GROUP
    mean = group_total(functools.reduce(jnp.add, means)) / members
    spread = functools.reduce(jnp.add, [(m - mean) * (m - mean) for m in means])
    total = group_total(functools.reduce(jnp.add, devs) + count * spread)
    return mean, lax.rsqrt(total / (members * count) + 1e-05)


def silu(values):
    half = 0.5 * values
    return half + half * jnp.tanh(half)


def row_sum(values):
    return values.reshape(-1, 8, values.shape[1]).sum(0)


def write_stats(st_ref, pivot, first, second, count):
    one = jnp.sum(first, axis=0, keepdims=True)
    two = jnp.sum(second, axis=0, keepdims=True)
    mean = pivot + one / count
    dev = two - one * one / count
    pad = jnp.zeros((6, mean.shape[1]), F32)
    st_ref[...] = jnp.concatenate([mean, dev, pad], axis=0)


def features_kernel(x_ref, head_ref, xt_ref, core_ref, far_ref, hf_ref, st_ref, scr, acc):
    step = pl.program_id(0)
    chans, rows, width = x_ref.shape
    even = (lax.axis_index("tile") & 1) == 0
    for part in range(width // 128):
        at = pl.ds(128 * part, 128)
        scr[part] = x_ref[:, :, at].astype(F32).reshape(chans * rows, 128)
        for r in range(rows):
            nat = scr[part, pl.ds(r, chans, stride=rows), :]
            hf_ref[r, :, at] = jnp.dot(head_ref[...], nat.astype(BF16), preferred_element_type=F32)
            turned = nat.T
            if part == 0 and r == 0:

                @pl.when(step == 0)
                def _():
                    middle = jnp.mean(turned, axis=0, keepdims=True)
                    acc[0] = jnp.broadcast_to(middle, acc.shape[1:])
                    acc[1] = jnp.zeros(acc.shape[1:], F32)
                    acc[2] = jnp.zeros(acc.shape[1:], F32)

                pivot = acc[0, 0:1]
            off = turned - pivot
            acc[1] += row_sum(off)
            acc[2] += row_sum(off * off)
            turned = turned.astype(BF16)
            xt_ref[r, at] = turned
            if r == 0:
                top = turned
        core_ref[at] = jnp.where(even, turned, top)
        far_ref[at] = jnp.where(even, top, turned)

    @pl.when(step == pl.num_programs(0) - 1)
    def _():
        write_stats(st_ref, acc[0, 0:1], acc[1], acc[2], pl.num_programs(0) * rows * width)


def features_call(x, head, block):
    chans, rows, width = x.shape
    edge = jax.ShapeDtypeStruct((width, chans), BF16)
    return pl.pallas_call(
        features_kernel,
        grid=(width // block,),
        out_shape=(
            jax.ShapeDtypeStruct((rows, width, chans), BF16),
            edge,
            edge,
            jax.ShapeDtypeStruct((rows, 8, width), F32),
            jax.ShapeDtypeStruct((8, chans), F32),
        ),
        in_specs=[
            pl.BlockSpec((chans, rows, block), lambda i: (0, 0, i)),
            pl.BlockSpec((8, chans), lambda i: (0, 0)),
        ],
        out_specs=(
            pl.BlockSpec((rows, block, chans), lambda i: (0, i, 0)),
            pl.BlockSpec((block, chans), lambda i: (i, 0)),
            pl.BlockSpec((block, chans), lambda i: (i, 0)),
            pl.BlockSpec((rows, 8, block), lambda i: (0, 0, i)),
            pl.BlockSpec((8, chans), lambda i: (0, 0)),
        ),
        scratch_shapes=[
            pltpu.VMEM((block // 128, chans * rows, 128), F32),
            pltpu.VMEM((3, 8, chans), F32),
        ],
        compiler_params=PARAMS,
        name="features",
    )(x, head)


def weights_kernel(first_ref, second_ref, head_ref, wt_ref, fold_ref):
    chans = first_ref.shape[1]
    wt_ref[...] = jnp.zeros(wt_ref.shape, BF16)
    for tap in range(9):
        turned = first_ref[tap].astype(F32).T.astype(BF16)
        for q in range(2):
            row, col = tap // 3 + q, tap % 3
            wt_ref[pl.ds((3 * row + col) * chans, chans), pl.ds(q * chans, chans)] = turned
    parts = []
    for tap in range(9):
        folded = jnp.dot(head_ref[...], second_ref[tap], preferred_element_type=F32)
        high = folded.astype(BF16).astype(F32)
        parts += [high[0:4], (folded - high)[0:4]]
    fold_ref[...] = jnp.concatenate(parts, axis=0).astype(BF16)


def weights_call(first, second, head):
    chans = first.shape[1]
    return pl.pallas_call(
        weights_kernel,
        out_shape=(
            jax.ShapeDtypeStruct((12 * chans, 2 * chans), BF16),
            jax.ShapeDtypeStruct((72, chans), BF16),
        ),
        in_specs=[VM] * 3,
        out_specs=(VM, VM),
        compiler_params=PARAMS,
        name="weights",
    )(first, second, head)


def first_kernel(
    block, x_ref, core_ref, far_ref, s0, s1, s2, s3, wt_ref, hid_ref, hcore_ref, hfar_ref, st_ref, act, buf
):
    rows, width, chans = x_ref.shape
    tile = lax.axis_index("tile")
    even = (tile & 1) == 0
    inner = ((tile == 1) | (tile == 2)).astype(F32)
    mean, scale = merged([s0[...], s1[...], s2[...], s3[...]], rows * width)
    shift = -mean * scale
    buf[pl.ds(0, 8), :] = jnp.zeros((8, chans), F32)
    buf[pl.ds(width + 8, 8), :] = jnp.zeros((8, chans), F32)
    size = 256

    def put(read, place, factor=None):
        def one(i, _):
            at = pl.multiple_of(i * size, size)
            value = silu(read(at).astype(F32) * scale + shift)
            if factor is not None:
                value = value * factor
            buf[pl.ds(at + 8, size), :] = value
            act[1, place, pl.ds(at, size), :] = value.astype(BF16)
            return 0

        lax.fori_loop(0, width // size, one, 0)

        def two(i, _):
            at = pl.multiple_of(i * size, size)
            act[0, place, pl.ds(at, size), :] = buf[pl.ds(at + 7, size), :].astype(BF16)
            act[2, place, pl.ds(at, size), :] = buf[pl.ds(at + 9, size), :].astype(BF16)
            return 0

        lax.fori_loop(0, width // size, two, 0)

    def own(r, _):
        put(lambda at: x_ref[r, pl.ds(at, size), :], r + 1)
        return 0

    lax.fori_loop(0, rows, own, 0)
    put(lambda at: core_ref[pl.ds(at, size), :], jnp.where(even, rows + 1, 0))
    put(lambda at: far_ref[pl.ds(at, size), :], jnp.where(even, 0, rows + 1), inner)

    per = width // block

    def mm(i, carry):
        pivot, one, two = carry
        pair = i // per
        at = pl.multiple_of((i % per) * block, block)
        left = jnp.concatenate(
            [act[s, 2 * pair + j, pl.ds(at, block), :] for j in range(4) for s in range(3)], axis=1
        )
        out = jnp.dot(left, wt_ref[...], preferred_element_type=F32)
        a, b = out[:, :chans], out[:, chans:]
        hid_ref[2 * pair, pl.ds(at, block), :] = a.astype(BF16)
        hid_ref[2 * pair + 1, pl.ds(at, block), :] = b.astype(BF16)
        pivot = jnp.where(i == 0, jnp.mean(a[0:8], axis=0, keepdims=True), pivot)
        a, b = a - pivot, b - pivot
        return pivot, one + row_sum(a + b), two + row_sum(a * a + b * b)

    zero = jnp.zeros((8, chans), F32)
    pivot, one, two = lax.fori_loop(0, (rows // 2) * per, mm, (zero[0:1], zero, zero))
    write_stats(st_ref, pivot, one, two, rows * width)

    def edges(i, _):
        at = pl.multiple_of(i * size, size)
        top, bottom = hid_ref[0, pl.ds(at, size), :], hid_ref[rows - 1, pl.ds(at, size), :]
        hcore_ref[pl.ds(at, size), :] = jnp.where(even, bottom, top)
        hfar_ref[pl.ds(at, size), :] = jnp.where(even, top, bottom)
        return 0

    lax.fori_loop(0, width // size, edges, 0)


def first_call(xt, core, far, stats, wt, block):
    rows, width, chans = xt.shape
    edge = jax.ShapeDtypeStruct((width, chans), BF16)
    return pl.pallas_call(
        functools.partial(first_kernel, block),
        out_shape=(
            jax.ShapeDtypeStruct(xt.shape, BF16),
            edge,
            edge,
            jax.ShapeDtypeStruct((8, chans), F32),
        ),
        in_specs=[VM] * 8,
        out_specs=(VM,) * 4,
        scratch_shapes=[
            pltpu.VMEM((3, rows + 2, width, chans), BF16),
            pltpu.VMEM((width + 16, chans), F32),
        ],
        compiler_params=PARAMS,
        name="first",
    )(xt, core, far, *stats, wt)


def step_factors(index):
    lane = lax.broadcasted_iota(jnp.int32, (8, 128), 1)
    steps = lane.astype(F32)
    upper = 800.0 ** (1.0 / 7.0)
    lower = 0.002 ** (1.0 / 7.0)
    root = upper + steps / 17.0 * (lower - upper)
    square = root * root
    sigmas = square * square * square * root
    sigma = jnp.sum(jnp.where(lane == index, sigmas, 0.0), axis=1, keepdims=True)
    follow = jnp.sum(jnp.where(lane == index + 1, sigmas, 0.0), axis=1, keepdims=True)
    sigma, follow = jnp.broadcast_to(sigma, lane.shape), jnp.broadcast_to(follow, lane.shape)
    hat = 1.25 * sigma
    spread = hat * hat + 0.25
    skip = 0.25 / spread
    gain = 0.5 * hat / jnp.sqrt(spread)
    rate = (follow - hat) / hat
    keep = 1.0 + rate - rate * skip
    return keep, keep * jnp.sqrt(hat * hat - sigma * sigma), -rate * gain


def second_kernel(
    hid_ref, core_ref, far_ref, s0, s1, s2, s3, fold_ref, hf_ref, state_ref, noise_ref, index_ref,
    next_ref, blocks_ref, act, taps, net,
):
    rows, width, chans = hid_ref.shape
    outs = state_ref.shape[0]
    tile = lax.axis_index("tile")
    even = (tile & 1) == 0
    inner = ((tile == 1) | (tile == 2)).astype(F32)
    mean, scale = merged([s0[...], s1[...], s2[...], s3[...]], rows * width)
    shift = -mean * scale
    size = 256

    def put(read, place, factor=None):
        def one(i, _):
            at = pl.multiple_of(i * size, size)
            value = silu(read(at).astype(F32) * scale + shift)
            if factor is not None:
                value = value * factor
            act[pl.ds(at, size), :] = value.astype(BF16)
            return 0

        lax.fori_loop(0, width // size, one, 0)
        taps[place] = lax.dot_general(
            fold_ref[...], act[...], (((1,), (1,)), ((), ())), preferred_element_type=F32
        )

    def own(r, _):
        put(lambda at: hid_ref[r, pl.ds(at, size), :], r + 1)
        return 0

    lax.fori_loop(0, rows, own, 0)
    put(lambda at: core_ref[pl.ds(at, size), :], jnp.where(even, rows + 1, 0))
    put(lambda at: far_ref[pl.ds(at, size), :], jnp.where(even, 0, rows + 1), inner)

    lane = lax.broadcasted_iota(jnp.int32, (8, width), 1)
    for r in range(rows):
        total = taps[r, 0:24] + taps[r + 1, 24:48] + taps[r + 2, 48:72]
        left = jnp.where(lane == 0, 0.0, pltpu.roll(total[0:8], 1, 1))
        right = jnp.where(lane == width - 1, 0.0, pltpu.roll(total[16:24], width - 1, 1))
        both = left + total[8:16] + right
        both = both[0:4] + both[4:8] + hf_ref[r, 0:4]
        for o in range(outs):
            net[o, r : r + 1, :] = both[o : o + 1]

    keep, stir, push = step_factors(index_ref[0])
    part = width // 16 // outs
    slot = lax.broadcasted_iota(jnp.int32, (rows, 128), 1) // part
    for t in range(width // 128):
        at = pl.ds(t * 128, 128)
        values = []
        for o in range(outs):
            value = keep * state_ref[o, :, at] + stir * noise_ref[o, :, at] + push * net[o, :, at]
            next_ref[o, :, at] = value
            values.append(value)
        for j in range(outs):
            mixed = values[j]
            for o in range(outs):
                if o != j:
                    moved = pltpu.roll(values[o], (part * (o - j)) % 128, 1)
                    mixed = jnp.where(slot == o, moved, mixed)
            blocks_ref[t * outs + j] = mixed


def second_call(hid, core, far, stats, fold, hf, state, noise, index):
    rows, width, chans = hid.shape
    return pl.pallas_call(
        second_kernel,
        out_shape=(
            jax.ShapeDtypeStruct(state.shape, F32),
            jax.ShapeDtypeStruct((width // 32, rows, 128), F32),
        ),
        in_specs=[VM] * 11 + [SM],
        out_specs=(VM, VM),
        scratch_shapes=[
            pltpu.VMEM((width, chans), BF16),
            pltpu.VMEM((rows + 2, 72, width), F32),
            pltpu.VMEM(state.shape, F32),
        ],
        compiler_params=PARAMS,
        name="second",
    )(hid, core, far, *stats, fold, hf, state, noise, index)


def spread_kernel(got_ref, reg_ref, target_ref, out_ref):
    members = got_ref.shape[0]
    zero = jnp.zeros(got_ref.shape[1:], F32)

    def add(m, carry):
        value = got_ref[m]
        return carry[0] + value, carry[1] + value * value

    first, second = lax.fori_loop(0, members, add, (zero, zero), unroll=8)
    slot = lax.broadcasted_iota(jnp.int32, zero.shape, 1) // 32
    target = zero
    for o in range(target_ref.shape[0]):
        target = jnp.where(slot == o, target_ref[o], target)
    mean = first / members
    var = second / members - mean * mean
    scale = jnp.sqrt(1.0 + target / (var + 1.0))
    offset = reg_ref[...] + mean - mean * scale

    def put(m, _):
        out_ref[m, 0] = scale
        out_ref[m, 1] = offset
        return 0

    lax.fori_loop(0, members, put, 0, unroll=8)


def spread_call(got, reg, target):
    members, rows, lanes = got.shape
    return pl.pallas_call(
        spread_kernel,
        out_shape=jax.ShapeDtypeStruct((members, 2, rows, lanes), F32),
        in_specs=[VM, VM, SM],
        out_specs=VM,
        compiler_params=PARAMS,
        name="spread",
    )(got, reg, target)


def field_kernel(blocks_ref, got_ref, out_ref):
    outs, rows, width = out_ref.shape
    part = 128 // outs
    slot = lax.broadcasted_iota(jnp.int32, (rows, 128), 1) // part
    for t in range(width // 128):
        values = [
            blocks_ref[t * outs + j] * got_ref[t * outs + j, 0] + got_ref[t * outs + j, 1]
            for j in range(outs)
        ]
        for o in range(outs):
            mixed = values[o]
            for j in range(outs):
                if j != o:
                    moved = pltpu.roll(values[j], (part * (j - o)) % 128, 1)
                    mixed = jnp.where(slot == j, moved, mixed)
            out_ref[o, :, pl.ds(t * 128, 128)] = mixed


def field_call(blocks, got, shape):
    return pl.pallas_call(
        field_kernel,
        out_shape=jax.ShapeDtypeStruct(shape, F32),
        in_specs=[VM, VM],
        out_specs=VM,
        compiler_params=PARAMS,
        name="field",
    )(blocks, got)


def exchange(core, far, stats):
    swap = lambda bits: [(i, i ^ bits) for i in range(TILES)]
    far = lax.ppermute(far, "tile", [(1, 2), (2, 1)])
    core = lax.ppermute(core, "tile", swap(1))
    return core, far, [stats] + [lax.ppermute(stats, "tile", swap(b)) for b in (1, 2, 3)]


def shards(
    features, residual_state, noise, regression_mean, step_index, conv_first, conv_second, head_weight, spread_target
):
    head = jnp.pad(head_weight, ((0, 8 - head_weight.shape[0]), (0, 0)))
    wt, fold = weights_call(conv_first, conv_second, head)
    xt, core, far, hf, stats = features_call(features[0], head, 256)
    core, far, stats = exchange(core, far, stats)
    hid, core, far, stats = first_call(xt, core, far, stats, wt, 1024)
    core, far, stats = exchange(core, far, stats)
    advanced, blocks = second_call(
        hid, core, far, stats, fold, hf, residual_state[0], noise[0], step_index
    )
    got = lax.all_to_all(blocks, "member", 0, 0, tiled=True)
    reg = jnp.transpose(regression_mean, (1, 0, 2)).reshape(got.shape[1:])
    sent = spread_call(got, reg, spread_target)
    got = lax.all_to_all(sent, "member", 0, 0, tiled=True)
    field = field_call(blocks, got, advanced.shape)
    return (field[None], advanced[None])


def solution(mesh):
    cells = P("member", None, "tile", None)
    return jax.shard_map(
        shards,
        mesh=mesh,
        in_specs=(cells, cells, cells, P(None, "tile", "member"), P(), P(), P(), P(), P()),
        out_specs=(cells, cells),
        check_vma=False,
    )
```

```python
import functools

import jax
import jax.numpy as jnp
from jax import lax
from jax.experimental import pallas as pl
from jax.experimental.pallas import tpu as pltpu
from jax.sharding import PartitionSpec as P

GROUP = 4
TILES = 4
F32, BF16 = jnp.float32, jnp.bfloat16
VM = pl.BlockSpec(memory_space=pltpu.VMEM)
SM = pl.BlockSpec(memory_space=pltpu.SMEM)


def limit(mib):
    return pltpu.CompilerParams(vmem_limit_bytes=mib * 1024 * 1024)


def group_total(row):
    lane = lax.broadcasted_iota(jnp.int32, row.shape, 1)
    size = row.shape[1]
    for step in (1, 2):
        up = pltpu.roll(row, step, 1)
        down = pltpu.roll(row, size - step, 1)
        row = row + jnp.where((lane & step) == 0, down, up)
    return row


def merged(parts, count):
    means = [p[0:1, :] for p in parts]
    devs = [p[1:2, :] for p in parts]
    members = len(parts) * GROUP
    mean = group_total(functools.reduce(jnp.add, means)) / members
    spread = functools.reduce(jnp.add, [(m - mean) * (m - mean) for m in means])
    total = group_total(functools.reduce(jnp.add, devs) + count * spread)
    return mean, lax.rsqrt(total / (members * count) + 1e-05)


def silu(values):
    half = 0.5 * values
    return half + half * jnp.tanh(half)


def row_sum(values):
    return values.reshape(-1, 8, values.shape[1]).sum(0)


def write_stats(st_ref, pivot, first, second, count):
    one = jnp.sum(first, axis=0, keepdims=True)
    two = jnp.sum(second, axis=0, keepdims=True)
    mean = pivot + one / count
    dev = two - one * one / count
    pad = jnp.zeros((6, mean.shape[1]), F32)
    st_ref[...] = jnp.concatenate([mean, dev, pad], axis=0)


def features_kernel(x_ref, xt_ref, core_ref, far_ref, st_ref, scr, acc):
    step = pl.program_id(0)
    chans, rows, width = x_ref.shape
    even = (lax.axis_index("tile") & 1) == 0
    for part in range(width // 128):
        at = pl.ds(128 * part, 128)
        scr[part] = x_ref[:, :, at].astype(F32).reshape(chans * rows, 128)
        one = two = jnp.zeros((8, chans), F32)
        for r in range(rows):
            turned = scr[part, pl.ds(r, chans, stride=rows), :].T
            if part == 0 and r == 0:

                @pl.when(step == 0)
                def _():
                    middle = jnp.mean(turned, axis=0, keepdims=True)
                    acc[0] = jnp.broadcast_to(middle, acc.shape[1:])
                    acc[1] = jnp.zeros(acc.shape[1:], F32)
                    acc[2] = jnp.zeros(acc.shape[1:], F32)

            if r == 0:
                pivot = acc[0, 0:1]
            off = turned - pivot
            one = one + row_sum(off)
            two = two + row_sum(off * off)
            turned = turned.astype(BF16)
            xt_ref[r, at] = turned
            if r == 0:
                top = turned
        acc[1] += one
        acc[2] += two
        core_ref[at] = jnp.where(even, turned, top)
        far_ref[at] = jnp.where(even, top, turned)

    @pl.when(step == pl.num_programs(0) - 1)
    def _():
        write_stats(st_ref, acc[0, 0:1], acc[1], acc[2], pl.num_programs(0) * rows * width)


def features_call(x, block):
    chans, rows, width = x.shape
    edge = jax.ShapeDtypeStruct((width, chans), BF16)
    return pl.pallas_call(
        features_kernel,
        grid=(width // block,),
        out_shape=(
            jax.ShapeDtypeStruct((rows, width, chans), BF16),
            edge,
            edge,
            jax.ShapeDtypeStruct((8, chans), F32),
        ),
        in_specs=[pl.BlockSpec((chans, rows, block), lambda i: (0, 0, i))],
        out_specs=(
            pl.BlockSpec((rows, block, chans), lambda i: (0, i, 0)),
            pl.BlockSpec((block, chans), lambda i: (i, 0)),
            pl.BlockSpec((block, chans), lambda i: (i, 0)),
            pl.BlockSpec((8, chans), lambda i: (0, 0)),
        ),
        scratch_shapes=[
            pltpu.VMEM((block // 128, chans * rows, 128), F32),
            pltpu.VMEM((3, 8, chans), F32),
        ],
        compiler_params=limit(16),
        name="features",
    )(x)


def step_factors(index):
    lane = lax.broadcasted_iota(jnp.int32, (8, 128), 1)
    steps = lane.astype(F32)
    upper = 800.0 ** (1.0 / 7.0)
    lower = 0.002 ** (1.0 / 7.0)
    root = upper + steps / 17.0 * (lower - upper)
    square = root * root
    sigmas = square * square * square * root
    sigma = jnp.sum(jnp.where(lane == index, sigmas, 0.0), axis=1, keepdims=True)
    follow = jnp.sum(jnp.where(lane == index + 1, sigmas, 0.0), axis=1, keepdims=True)
    sigma, follow = jnp.broadcast_to(sigma, lane.shape), jnp.broadcast_to(follow, lane.shape)
    hat = 1.25 * sigma
    spread = hat * hat + 0.25
    skip = 0.25 / spread
    gain = 0.5 * hat / jnp.sqrt(spread)
    rate = (follow - hat) / hat
    keep = 1.0 + rate - rate * skip
    return keep, keep * jnp.sqrt(hat * hat - sigma * sigma), -rate * gain


def weights_kernel(first_ref, second_ref, head_ref, wt_ref, fold_ref):
    chans = first_ref.shape[1]
    wt_ref[...] = jnp.zeros(wt_ref.shape, BF16)
    for tap in range(9):
        turned = first_ref[tap].astype(F32).T.astype(BF16)
        for q in range(2):
            row, col = tap // 3 + q, tap % 3
            wt_ref[pl.ds((3 * row + col) * chans, chans), pl.ds(q * chans, chans)] = turned
    head = jnp.concatenate([head_ref[...].astype(F32)] * 2, axis=0).astype(BF16)
    low = lax.broadcasted_iota(jnp.int32, (8, chans), 0) >= 4
    lines = []
    for row in range(3):
        parts = []
        for col in range(3):
            folded = jnp.dot(head, second_ref[3 * row + col], preferred_element_type=F32)
            high = folded.astype(BF16).astype(F32)
            parts.append(jnp.where(low, folded - high, high))
        lines.append(jnp.concatenate(parts, axis=0))
    none = jnp.zeros_like(lines[0])
    left = jnp.concatenate([lines[2], lines[1], lines[0], none], axis=0)
    right = jnp.concatenate([none, lines[2], lines[1], lines[0]], axis=0)
    fold_ref[...] = jnp.concatenate([left, right], axis=1).astype(BF16)


def weights_call(first, second, head):
    chans = first.shape[1]
    return pl.pallas_call(
        weights_kernel,
        out_shape=(
            jax.ShapeDtypeStruct((12 * chans, 2 * chans), BF16),
            jax.ShapeDtypeStruct((96, 2 * chans), BF16),
        ),
        in_specs=[VM] * 3,
        out_specs=(VM, VM),
        compiler_params=limit(16),
        cost_estimate=pl.CostEstimate(flops=1 << 22, bytes_accessed=1 << 21, transcendentals=0),
        name="weights",
    )(first, second, head)


def turned_on():
    tile = lax.axis_index("tile")
    even = (tile & 1) == 0
    inner = ((tile == 1) | (tile == 2)).astype(F32)
    return even, jnp.where(even, inner, 1.0), jnp.where(even, 1.0, inner)


def norm_factors(refs, count):
    mean, scale = merged([ref[...] for ref in refs], count)
    return scale, -mean * scale


def fill(act, buf, value, at, size):
    buf[pl.ds(at + 8, size), :] = value
    act[1, pl.ds(at, size), :] = value.astype(BF16)


def fill_sides(act, buf, at, size):
    act[0, pl.ds(at, size), :] = buf[pl.ds(at + 7, size), :].astype(BF16)
    act[2, pl.ds(at, size), :] = buf[pl.ds(at + 9, size), :].astype(BF16)


def clear_ends(buf):
    size, chans = buf.shape
    buf[pl.ds(0, 8), :] = jnp.zeros((8, chans), F32)
    buf[pl.ds(size - 8, 8), :] = jnp.zeros((8, chans), F32)


def two_rows(acts, wt_ref, at, block):
    left = jnp.concatenate([act[s, pl.ds(at, block), :] for act in acts for s in range(3)], axis=1)
    out = jnp.dot(left, wt_ref[...], preferred_element_type=F32)
    chans = out.shape[1] // 2
    return out[:, :chans], out[:, chans:]


def inner_kernel(block, x_ref, s0, s1, s2, s3, wt_ref, hid_ref, sum_ref, *rest):
    rows, width, chans = x_ref.shape
    acts, bufs = rest[:rows], rest[rows:]
    scale, shift = norm_factors([s0, s1, s2, s3], rows * width)
    for buf in bufs:
        clear_ends(buf)

    def centre(row, at, size):
        value = silu(x_ref[row, pl.ds(at, size), :].astype(F32) * scale + shift)
        fill(acts[row], bufs[row % 2], value, at, size)

    def sides(row, at, size):
        fill_sides(acts[row], bufs[row % 2], at, size)

    for row in range(1, 5):
        centre(row, 0, width)
        sides(row, 0, width)
    one = two = jnp.zeros((8, chans), F32)
    pivot = None
    for pair, fresh in ((0, (5, 6)), (1, (7, 0))):
        for at in range(0, width, block):
            a, b = two_rows(acts[2 * pair + 1 : 2 * pair + 5], wt_ref, at, block)
            for row in fresh:
                centre(row, at, block)
                if at > 0:
                    sides(row, at - block, block)
            hid_ref[2 * pair, pl.ds(at, block), :] = a.astype(BF16)
            hid_ref[2 * pair + 1, pl.ds(at, block), :] = b.astype(BF16)
            if pivot is None:
                pivot = jnp.mean(a[0:8], axis=0, keepdims=True)
            a, b = a - pivot, b - pivot
            one = one + row_sum(a + b)
            two = two + row_sum(a * a + b * b)
        for row in fresh:
            sides(row, width - block, block)
    sum_ref[0] = jnp.broadcast_to(pivot, one.shape)
    sum_ref[1] = one
    sum_ref[2] = two


def inner_call(xt, stats, wt, block):
    rows, width, chans = xt.shape
    act = jax.ShapeDtypeStruct((3, width, chans), BF16)
    hid, sums, *acts = pl.pallas_call(
        functools.partial(inner_kernel, block),
        out_shape=(
            jax.ShapeDtypeStruct((rows - 4, width, chans), BF16),
            jax.ShapeDtypeStruct((3, 8, chans), F32),
        )
        + (act,) * rows,
        in_specs=[VM] * 6,
        out_specs=(VM,) * (rows + 2),
        scratch_shapes=[pltpu.VMEM((width + 16, chans), F32)] * 2,
        compiler_params=limit(26),
        cost_estimate=pl.CostEstimate(
            flops=12 * rows * width * chans * chans * 2, bytes_accessed=1 << 22, transcendentals=xt.size
        ),
        name="inner",
    )(xt, *stats, wt)
    return hid, sums, acts


def outer_kernel(block, *refs):
    acts, refs = list(refs[:6]), refs[6:]
    core_ref, far_ref, s0, s1, s2, s3, sum_ref, wt_ref, hid_ref, hcore_ref, hfar_ref, st_ref, top, bottom, b0, b1 = refs
    width, chans = core_ref.shape
    rows = hid_ref.shape[0] + 4
    even, top_on, bottom_on = turned_on()
    scale, shift = norm_factors([s0, s1, s2, s3], rows * width)

    def halo(act, buf, pick, factor, at):
        clear_ends(buf)
        value = silu(pick(pl.ds(at, block)).astype(F32) * scale + shift) * factor
        fill(act, buf, value, at, block)
        if at > 0:
            fill_sides(act, buf, at - block, block)
        if at + block == width:
            fill_sides(act, buf, at, block)

    upper = lambda at: jnp.where(even, far_ref[at, :], core_ref[at, :])
    lower = lambda at: jnp.where(even, core_ref[at, :], far_ref[at, :])
    for at in range(0, width, block):
        halo(top, b0, upper, top_on, at)
    pivot, one, two = sum_ref[0, 0:1], sum_ref[1], sum_ref[2]
    groups = ([top] + acts[:3], acts[3:] + [bottom])
    for pair, group in enumerate(groups):
        for at in range(0, width, block):
            a, b = two_rows(group, wt_ref, at, block)
            if pair == 0:
                halo(bottom, b1, lower, bottom_on, at)
            high, low = a.astype(BF16), b.astype(BF16)
            hid_ref[2 * pair, pl.ds(at, block), :] = high
            hid_ref[2 * pair + 1, pl.ds(at, block), :] = low
            if pair == 0:
                hcore_ref[pl.ds(at, block), :] = high
            else:
                first = hcore_ref[pl.ds(at, block), :]
                hcore_ref[pl.ds(at, block), :] = jnp.where(even, low, first)
                hfar_ref[pl.ds(at, block), :] = jnp.where(even, first, low)
            a, b = a - pivot, b - pivot
            one = one + row_sum(a + b)
            two = two + row_sum(a * a + b * b)
    write_stats(st_ref, pivot, one, two, rows * width)


def outer_call(acts, core, far, stats, sums, wt, block):
    width, chans = core.shape
    edge = jax.ShapeDtypeStruct((width, chans), BF16)
    act = pltpu.VMEM((3, width, chans), BF16)
    return pl.pallas_call(
        functools.partial(outer_kernel, block),
        out_shape=(
            jax.ShapeDtypeStruct((4, width, chans), BF16),
            edge,
            edge,
            jax.ShapeDtypeStruct((8, chans), F32),
        ),
        in_specs=[VM] * 14,
        out_specs=(VM,) * 4,
        scratch_shapes=[act] * 2 + [pltpu.VMEM((width + 16, chans), F32)] * 2,
        compiler_params=limit(20),
        name="outer",
    )(*acts[:3], *acts[-3:], core, far, *stats, sums, wt)


def turn_quarters(values, slot):
    out = []
    for j in range(4):
        mixed = values[j]
        for k in range(4):
            if k != j:
                moved = pltpu.roll(values[k], (32 * (k - j)) % 128, 1)
                mixed = jnp.where(slot == k, moved, mixed)
        out.append(mixed)
    return out


def taps_kernel(x_ref, mid_ref, rim_ref, s0, s1, s2, s3, fold_ref, head_ref, sum_ref, *rest):
    half, width, chans = mid_ref.shape
    rows = 2 * half
    acts, taps = rest[:half], rest[half]
    scale, shift = norm_factors([s0, s1, s2, s3], rows * width)
    head = head_ref[...].astype(F32)
    head = jnp.concatenate([head, jnp.zeros_like(head)], axis=0)
    none = jnp.zeros_like(head)
    head = jnp.concatenate(
        [jnp.concatenate([head, none], axis=1), jnp.concatenate([none, head], axis=1)], axis=0
    ).astype(BF16)
    direct = []
    for pair in range(half):
        features = jnp.concatenate([x_ref[2 * pair], x_ref[2 * pair + 1]], axis=1)
        direct.append(
            lax.dot_general(head, features, (((1,), (1,)), ((), ())), preferred_element_type=F32)
        )
        for side in range(2):
            row = 2 * pair + side
            if row < 2:
                value = rim_ref[row]
            elif row < rows - 2:
                value = mid_ref[row - 2]
            else:
                value = rim_ref[row - half]
            value = silu(value.astype(F32) * scale + shift)
            acts[pair][:, pl.ds(side * chans, chans)] = value.astype(BF16)
        taps[pair] = lax.dot_general(
            fold_ref[...], acts[pair][...], (((1,), (1,)), ((), ())), preferred_element_type=F32
        )
    for pair in range(half):
        total = taps[pair, 24:48]
        if pair > 0:
            total = total + taps[pair - 1, 72:96]
        sum_ref[2 * pair] = total
        sum_ref[2 * pair, 8:16] += direct[pair][0:8]
        total = taps[pair, 48:72]
        if pair + 1 < half:
            total = total + taps[pair + 1, 0:24]
        sum_ref[2 * pair + 1] = total
        sum_ref[2 * pair + 1, 8:16] += direct[pair][8:16]


def taps_call(xt, mid, rim, stats, fold, head):
    half, width, chans = mid.shape
    return pl.pallas_call(
        taps_kernel,
        out_shape=jax.ShapeDtypeStruct((2 * half, 24, width), F32),
        in_specs=[VM] * 9,
        out_specs=VM,
        scratch_shapes=[pltpu.VMEM((width, 2 * chans), BF16)] * half + [pltpu.VMEM((half, 96, width), F32)],
        compiler_params=limit(24),
        cost_estimate=pl.CostEstimate(
            flops=768 * width * chans * half * 8, bytes_accessed=1 << 22, transcendentals=2 * mid.size
        ),
        name="taps",
    )(xt, mid, rim, *stats, fold, head)


def step_kernel(
    core_ref, far_ref, s0, s1, s2, s3, fold_ref, sum_ref, state_ref, noise_ref, index_ref,
    next_ref, blocks_ref, act, net,
):
    width, chans = core_ref.shape
    rows = sum_ref.shape[0]
    outs = state_ref.shape[0]
    even, top_on, bottom_on = turned_on()
    scale, shift = norm_factors([s0, s1, s2, s3], rows * width)
    upper = jnp.where(even, far_ref[...], core_ref[...])
    lower = jnp.where(even, core_ref[...], far_ref[...])
    upper = silu(upper.astype(F32) * scale + shift) * top_on
    lower = silu(lower.astype(F32) * scale + shift) * bottom_on
    act[:, pl.ds(0, chans)] = upper.astype(BF16)
    act[:, pl.ds(chans, chans)] = lower.astype(BF16)
    none = jnp.zeros((24, chans), BF16)
    ends = jnp.concatenate(
        [
            jnp.concatenate([fold_ref[72:96, chans:], none], axis=1),
            jnp.concatenate([none, fold_ref[0:24, :chans]], axis=1),
        ],
        axis=0,
    )
    ends = lax.dot_general(ends, act[...], (((1,), (1,)), ((), ())), preferred_element_type=F32)
    lane = lax.broadcasted_iota(jnp.int32, (8, width), 1)
    for r in range(rows):
        total = sum_ref[r]
        if r == 0:
            total = total + ends[0:24]
        if r == rows - 1:
            total = total + ends[24:48]
        left = jnp.where(lane == 0, 0.0, pltpu.roll(total[0:8], 1, 1))
        right = jnp.where(lane == width - 1, 0.0, pltpu.roll(total[16:24], width - 1, 1))
        both = left + total[8:16] + right
        both = both[0:4] + both[4:8]
        for o in range(outs):
            net[o, r : r + 1, :] = both[o : o + 1]

    keep, stir, push = step_factors(index_ref[0])
    quarter = width // 512
    for t in range(width // 128):
        at = pl.ds(t * 128, 128)
        for o in range(outs):
            direct = keep * state_ref[o, :, at] + stir * noise_ref[o, :, at]
            next_ref[o, :, at] = direct + push * net[o, :, at]
    slot = lax.broadcasted_iota(jnp.int32, (rows, 128), 1) // 32
    for t in range(quarter):
        for o in range(outs):
            values = [next_ref[o, :, pl.ds((quarter * k + t) * 128, 128)] for k in range(4)]
            for j, mixed in enumerate(turn_quarters(values, slot)):
                blocks_ref[4 * t + j, o] = mixed


def step_call(core, far, stats, fold, sums, state, noise, index):
    width, chans = core.shape
    rows = sums.shape[0]
    return pl.pallas_call(
        step_kernel,
        out_shape=(
            jax.ShapeDtypeStruct(state.shape, F32),
            jax.ShapeDtypeStruct((width // 128, state.shape[0], rows, 128), F32),
        ),
        in_specs=[VM] * 10 + [SM],
        out_specs=(VM, VM),
        scratch_shapes=[pltpu.VMEM((width, 2 * chans), BF16), pltpu.VMEM(state.shape, F32)],
        compiler_params=limit(12),
        name="step",
    )(core, far, *stats, fold, sums, state, noise, index)


def sums_kernel(got_ref, reg_ref, out_ref):
    count = got_ref.shape[0]
    shape = got_ref.shape[2:]
    own = lax.broadcasted_iota(jnp.int32, shape, 1) // 32 == lax.axis_index("member") // count
    for o in range(got_ref.shape[1]):
        first = got_ref[0, o]
        second = first * first
        for m in range(1, count):
            value = got_ref[m, o]
            first = first + value
            second = second + value * value
        out_ref[0, o] = first
        out_ref[1, o] = second
        out_ref[2, o] = jnp.where(own, reg_ref[o], 0.0)


def sums_call(got, reg):
    return pl.pallas_call(
        sums_kernel,
        out_shape=jax.ShapeDtypeStruct((3,) + got.shape[1:], F32),
        in_specs=[VM, VM],
        out_specs=VM,
        compiler_params=limit(8),
        name="sums",
    )(got, reg)


def spread_kernel(members, one_ref, two_ref, target_ref, out_ref):
    copies, _, outs = out_ref.shape[:3]
    for o in range(outs):
        mean = (one_ref[0, o] + two_ref[0, o]) / members
        var = (one_ref[1, o] + two_ref[1, o]) / members - mean * mean
        scale = jnp.sqrt(1.0 + target_ref[o] / (var + 1.0))
        offset = one_ref[2, o] + two_ref[2, o] + mean - mean * scale
        for k in range(copies):
            out_ref[k, 0, o] = scale
            out_ref[k, 1, o] = offset


def spread_call(one, two, target, copies, members):
    return pl.pallas_call(
        functools.partial(spread_kernel, members),
        out_shape=jax.ShapeDtypeStruct((copies, 2) + one.shape[1:], F32),
        in_specs=[VM, VM, SM],
        out_specs=VM,
        compiler_params=limit(8),
        name="spread",
    )(one, two, target)


def field_kernel(blocks_ref, got_ref, out_ref):
    outs, rows, width = out_ref.shape
    quarter = width // 512
    slot = lax.broadcasted_iota(jnp.int32, (rows, 128), 1) // 32
    for t in range(quarter):
        for o in range(outs):
            values = [
                blocks_ref[4 * t + j, o] * got_ref[4 * t + j, 0, o] + got_ref[4 * t + j, 1, o] for j in range(4)
            ]
            for k, mixed in enumerate(turn_quarters(values, slot)):
                out_ref[o, :, pl.ds((quarter * k + t) * 128, 128)] = mixed


def field_call(blocks, got, shape):
    return pl.pallas_call(
        field_kernel,
        out_shape=jax.ShapeDtypeStruct(shape, F32),
        in_specs=[VM, VM],
        out_specs=VM,
        compiler_params=limit(8),
        name="field",
    )(blocks, got)


def exchange(core, far, stats):
    swap = lambda bits: [(i, i ^ bits) for i in range(TILES)]
    parts = [stats] + [lax.ppermute(stats, "tile", swap(b)) for b in (1, 2, 3)]
    far = lax.ppermute(far, "tile", [(1, 2), (2, 1)])
    core = lax.ppermute(core, "tile", swap(1))
    return core, far, parts


def shards(
    features, residual_state, noise, regression_mean, step_index, conv_first, conv_second, head_weight, spread_target
):
    member = pltpu.with_memory_space_constraint(features[0], pltpu.HBM)
    xt, core, far, stats = features_call(member, 256)
    core, far, stats = exchange(core, far, stats)
    wt, fold = weights_call(conv_first, conv_second, head_weight)
    mid, sums, acts = inner_call(xt, stats, wt, 1024)
    rim, core, far, stats = outer_call(acts, core, far, stats, sums, wt, 1024)
    core, far, stats = exchange(core, far, stats)
    sums = taps_call(xt, mid, rim, stats, fold, head_weight)
    advanced, blocks = step_call(
        core, far, stats, fold, sums, residual_state[0], noise[0], step_index
    )
    members = lax.axis_size("member")
    size = blocks.shape[0]
    runs = [list(range(i, i + size)) for i in range(0, members, size)]
    got = lax.all_to_all(blocks, "member", 0, 0, tiled=True, axis_index_groups=runs)
    reg = jnp.tile(regression_mean, (1, 1, 4))
    sums = sums_call(got, reg)
    sums = sums + lax.ppermute(sums, "member", [(i, i ^ size) for i in range(members)])
    other = lax.ppermute(sums, "member", [(i, i ^ (3 * size)) for i in range(members)])
    sent = spread_call(sums, other, spread_target, size, members)
    got = lax.all_to_all(sent, "member", 0, 0, tiled=True, axis_index_groups=runs)
    field = field_call(blocks, got, advanced.shape)
    return (field[None], advanced[None])


def solution(mesh):
    cells = P("member", None, "tile", None)
    return jax.shard_map(
        shards,
        mesh=mesh,
        in_specs=(cells, cells, cells, P(None, "tile", "member"), P(), P(), P(), P(), P()),
        out_specs=(cells, cells),
        check_vma=False,
    )
```

```python
import functools

import jax
import jax.numpy as jnp
from jax import lax
from jax.experimental import pallas as pl
from jax.experimental.pallas import tpu as pltpu
from jax.sharding import PartitionSpec as P

GROUP = 4
TILES = 4
F32, BF16 = jnp.float32, jnp.bfloat16
VM = pl.BlockSpec(memory_space=pltpu.VMEM)
SM = pl.BlockSpec(memory_space=pltpu.SMEM)


def limit(mib):
    return pltpu.CompilerParams(vmem_limit_bytes=mib * 1024 * 1024)


def group_total(row):
    lane = lax.broadcasted_iota(jnp.int32, row.shape, 1)
    size = row.shape[1]
    for step in (1, 2):
        up = pltpu.roll(row, step, 1)
        down = pltpu.roll(row, size - step, 1)
        row = row + jnp.where((lane & step) == 0, down, up)
    return row


def merged(parts, count):
    means = [p[0:1, :] for p in parts]
    devs = [p[1:2, :] for p in parts]
    members = len(parts) * GROUP
    mean = group_total(functools.reduce(jnp.add, means)) / members
    spread = functools.reduce(jnp.add, [(m - mean) * (m - mean) for m in means])
    total = group_total(functools.reduce(jnp.add, devs) + count * spread)
    return mean, lax.rsqrt(total / (members * count) + 1e-05)


def silu(values):
    half = 0.5 * values
    return half + half * jnp.tanh(half)


def row_sum(values):
    return values.reshape(-1, 8, values.shape[1]).sum(0)


def write_stats(st_ref, pivot, first, second, count):
    one = jnp.sum(first, axis=0, keepdims=True)
    two = jnp.sum(second, axis=0, keepdims=True)
    mean = pivot + one / count
    dev = two - one * one / count
    pad = jnp.zeros((6, mean.shape[1]), F32)
    st_ref[...] = jnp.concatenate([mean, dev, pad], axis=0)


def features_kernel(x_ref, xt_ref, core_ref, far_ref, st_ref, scr, acc):
    step = pl.program_id(0)
    chans, rows, width = x_ref.shape
    even = (lax.axis_index("tile") & 1) == 0
    for part in range(width // 128):
        at = pl.ds(128 * part, 128)
        scr[part] = x_ref[:, :, at].astype(F32).reshape(chans * rows, 128)
        one = two = jnp.zeros((8, chans), F32)
        for r in range(rows):
            turned = scr[part, pl.ds(r, chans, stride=rows), :].T
            if part == 0 and r == 0:

                @pl.when(step == 0)
                def _():
                    middle = jnp.mean(turned, axis=0, keepdims=True)
                    acc[0] = jnp.broadcast_to(middle, acc.shape[1:])
                    acc[1] = jnp.zeros(acc.shape[1:], F32)
                    acc[2] = jnp.zeros(acc.shape[1:], F32)

            if r == 0:
                pivot = acc[0, 0:1]
            off = turned - pivot
            one = one + row_sum(off)
            two = two + row_sum(off * off)
            turned = turned.astype(BF16)
            xt_ref[jnp.where(even, r, rows - 1 - r), at] = turned
            if r == 0:
                top = turned
        acc[1] += one
        acc[2] += two
        core_ref[at] = jnp.where(even, turned, top)
        far_ref[at] = jnp.where(even, top, turned)

    @pl.when(step == pl.num_programs(0) - 1)
    def _():
        write_stats(st_ref, acc[0, 0:1], acc[1], acc[2], pl.num_programs(0) * rows * width)


def features_call(x, block):
    chans, rows, width = x.shape
    edge = jax.ShapeDtypeStruct((width, chans), BF16)
    return pl.pallas_call(
        features_kernel,
        grid=(width // block,),
        out_shape=(
            jax.ShapeDtypeStruct((rows, width, chans), BF16),
            edge,
            edge,
            jax.ShapeDtypeStruct((8, chans), F32),
        ),
        in_specs=[pl.BlockSpec((chans, rows, block), lambda i: (0, 0, i))],
        out_specs=(
            pl.BlockSpec((rows, block, chans), lambda i: (0, i, 0)),
            pl.BlockSpec((block, chans), lambda i: (i, 0)),
            pl.BlockSpec((block, chans), lambda i: (i, 0)),
            pl.BlockSpec((8, chans), lambda i: (0, 0)),
        ),
        scratch_shapes=[
            pltpu.VMEM((block // 128, chans * rows, 128), F32),
            pltpu.VMEM((3, 8, chans), F32),
        ],
        compiler_params=limit(16),
        name="features",
    )(x)


def step_factors(index):
    lane = lax.broadcasted_iota(jnp.int32, (8, 128), 1)
    steps = lane.astype(F32)
    upper = 800.0 ** (1.0 / 7.0)
    lower = 0.002 ** (1.0 / 7.0)
    root = upper + steps / 17.0 * (lower - upper)
    square = root * root
    sigmas = square * square * square * root
    sigma = jnp.sum(jnp.where(lane == index, sigmas, 0.0), axis=1, keepdims=True)
    follow = jnp.sum(jnp.where(lane == index + 1, sigmas, 0.0), axis=1, keepdims=True)
    sigma, follow = jnp.broadcast_to(sigma, lane.shape), jnp.broadcast_to(follow, lane.shape)
    hat = 1.25 * sigma
    spread = hat * hat + 0.25
    skip = 0.25 / spread
    gain = 0.5 * hat / jnp.sqrt(spread)
    rate = (follow - hat) / hat
    keep = 1.0 + rate - rate * skip
    return keep, keep * jnp.sqrt(hat * hat - sigma * sigma), -rate * gain


def place(even, tap):
    return jnp.where(even, tap, 3 * (2 - tap // 3) + tap % 3)


def weights_kernel(first_ref, second_ref, head_ref, wt_ref, fold_ref):
    chans = first_ref.shape[1]
    even = (lax.axis_index("tile") & 1) == 0
    wt_ref[...] = jnp.zeros(wt_ref.shape, BF16)
    for tap in range(9):
        turned = first_ref[place(even, tap)].astype(F32).T.astype(BF16)
        for q in range(2):
            row, col = tap // 3 + q, tap % 3
            wt_ref[pl.ds((3 * row + col) * chans, chans), pl.ds(q * chans, chans)] = turned
    head = jnp.concatenate([head_ref[...].astype(F32)] * 2, axis=0).astype(BF16)
    low = lax.broadcasted_iota(jnp.int32, (8, chans), 0) >= 4
    lines = []
    for row in range(3):
        parts = []
        for col in range(3):
            tap = second_ref[place(even, 3 * row + col)]
            folded = jnp.dot(head, tap, preferred_element_type=F32)
            high = folded.astype(BF16).astype(F32)
            parts.append(jnp.where(low, folded - high, high))
        lines.append(jnp.concatenate(parts, axis=0))
    none = jnp.zeros_like(lines[0])
    left = jnp.concatenate([lines[2], lines[1], lines[0], none], axis=0)
    right = jnp.concatenate([none, lines[2], lines[1], lines[0]], axis=0)
    fold_ref[...] = jnp.concatenate([left, right], axis=1).astype(BF16)


def weights_call(first, second, head):
    chans = first.shape[1]
    return pl.pallas_call(
        weights_kernel,
        out_shape=(
            jax.ShapeDtypeStruct((12 * chans, 2 * chans), BF16),
            jax.ShapeDtypeStruct((96, 2 * chans), BF16),
        ),
        in_specs=[VM] * 3,
        out_specs=(VM, VM),
        compiler_params=limit(16),
        cost_estimate=pl.CostEstimate(flops=1 << 22, bytes_accessed=1 << 21, transcendentals=0),
        name="weights",
    )(first, second, head)


def norm_factors(refs, count):
    mean, scale = merged([ref[...] for ref in refs], count)
    return scale, -mean * scale


def fill(act, buf, value, at, size):
    buf[pl.ds(at + 8, size), :] = value
    act[1, pl.ds(at, size), :] = value.astype(BF16)


def fill_sides(act, buf, at, size):
    act[0, pl.ds(at, size), :] = buf[pl.ds(at + 7, size), :].astype(BF16)
    act[2, pl.ds(at, size), :] = buf[pl.ds(at + 9, size), :].astype(BF16)


def clear_ends(buf):
    size, chans = buf.shape
    buf[pl.ds(0, 8), :] = jnp.zeros((8, chans), F32)
    buf[pl.ds(size - 8, 8), :] = jnp.zeros((8, chans), F32)


def two_rows(acts, wt_ref, at, block):
    left = jnp.concatenate([act[s, pl.ds(at, block), :] for act in acts for s in range(3)], axis=1)
    out = jnp.dot(left, wt_ref[...], preferred_element_type=F32)
    chans = out.shape[1] // 2
    return out[:, :chans], out[:, chans:]


def join(acts, wt_ref, hid_ref, lines, block, fresh, carry):
    width = hid_ref.shape[1]
    pivot, one, two = carry
    for at in range(0, width, block):
        a, b = two_rows(acts, wt_ref, at, block)
        for act, buf, read in fresh:
            fill(act, buf, read(at, block), at, block)
            if at > 0:
                fill_sides(act, buf, at - block, block)
        hid_ref[lines[0], pl.ds(at, block), :] = a.astype(BF16)
        hid_ref[lines[1], pl.ds(at, block), :] = b.astype(BF16)
        if pivot is None:
            pivot = jnp.mean(a[0:8], axis=0, keepdims=True)
        a, b = a - pivot, b - pivot
        one = one + row_sum(a + b)
        two = two + row_sum(a * a + b * b)
    for act, buf, read in fresh:
        fill_sides(act, buf, width - block, block)
    return pivot, one, two


def inner_kernel(block, x_ref, core_ref, s0, s1, s2, s3, wt_ref, hid_ref, sum_ref, *rest):
    rows, width, chans = x_ref.shape
    acts, bufs = rest[: rows + 1], rest[rows + 1 :]
    scale, shift = norm_factors([s0, s1, s2, s3], rows * width)
    for buf in bufs:
        clear_ends(buf)

    def line(row):
        def read(at, size):
            span = pl.ds(at, size)
            value = core_ref[span, :] if row == rows else x_ref[row, span, :]
            return silu(value.astype(F32) * scale + shift)

        return acts[row], bufs[row % 2], read

    for row in range(1, 5):
        act, buf, read = line(row)
        fill(act, buf, read(0, width), 0, width)
        fill_sides(act, buf, 0, width)
    zero = jnp.zeros((8, chans), F32)
    carry = (None, zero, zero)
    for pair, fresh in ((0, (5, 6)), (1, (7, 8)), (2, (0,))):
        group = acts[2 * pair + 1 : 2 * pair + 5]
        lines = (2 * pair, 2 * pair + 1)
        carry = join(group, wt_ref, hid_ref, lines, block, [line(row) for row in fresh], carry)
    pivot, one, two = carry
    sum_ref[0] = jnp.broadcast_to(pivot, one.shape)
    sum_ref[1] = one
    sum_ref[2] = two


def inner_call(xt, core, stats, wt, block):
    rows, width, chans = xt.shape
    act = jax.ShapeDtypeStruct((3, width, chans), BF16)
    hid, sums, *acts = pl.pallas_call(
        functools.partial(inner_kernel, block),
        out_shape=(
            jax.ShapeDtypeStruct((rows - 2, width, chans), BF16),
            jax.ShapeDtypeStruct((3, 8, chans), F32),
            act,
            act,
            act,
        ),
        in_specs=[VM] * 7,
        out_specs=(VM,) * 5,
        scratch_shapes=[pltpu.VMEM(act.shape, BF16)] * (rows - 2)
        + [pltpu.VMEM((width + 16, chans), F32)] * 2,
        compiler_params=limit(28),
        cost_estimate=pl.CostEstimate(
            flops=24 * rows * width * chans * chans, bytes_accessed=1 << 22, transcendentals=xt.size
        ),
        name="inner",
    )(xt, core, *stats, wt)
    return hid, sums, acts


def outer_kernel(block, far_ref, a0, a1, a2, s0, s1, s2, s3, sum_ref, wt_ref, hid_ref, st_ref, act, buf):
    width, chans = far_ref.shape
    tile = lax.axis_index("tile")
    linked = ((tile == 1) | (tile == 2)).astype(F32)
    count = TILES * 2 * width
    scale, shift = norm_factors([s0, s1, s2, s3], count)
    clear_ends(buf)
    for at in range(0, width, block):
        value = silu(far_ref[pl.ds(at, block), :].astype(F32) * scale + shift) * linked
        fill(act, buf, value, at, block)
        if at > 0:
            fill_sides(act, buf, at - block, block)
    fill_sides(act, buf, width - block, block)
    carry = (sum_ref[0, 0:1], sum_ref[1], sum_ref[2])
    pivot, one, two = join([act, a0, a1, a2], wt_ref, hid_ref, (0, 1), block, [], carry)
    write_stats(st_ref, pivot, one, two, count)


def outer_call(acts, far, stats, sums, wt, block):
    width, chans = far.shape
    return pl.pallas_call(
        functools.partial(outer_kernel, block),
        out_shape=(
            jax.ShapeDtypeStruct((2, width, chans), BF16),
            jax.ShapeDtypeStruct((8, chans), F32),
        ),
        in_specs=[VM] * 10,
        out_specs=(VM,) * 2,
        scratch_shapes=[pltpu.VMEM((3, width, chans), BF16), pltpu.VMEM((width + 16, chans), F32)],
        compiler_params=limit(12),
        name="outer",
    )(far, *acts, *stats, sums, wt)


def turn_quarters(values, slot):
    low, right = slot < 2, (slot & 1) == 0
    halves = []
    for a, b in ((values[0], values[2]), (values[1], values[3])):
        moved = pltpu.roll(jnp.where(low, b, a), 64, 1)
        halves.append((jnp.where(low, a, moved), jnp.where(low, moved, b)))
    out = [None] * 4
    for k in range(2):
        a, b = halves[0][k], halves[1][k]
        out[2 * k] = jnp.where(right, a, pltpu.roll(b, 32, 1))
        out[2 * k + 1] = jnp.where(right, pltpu.roll(a, 96, 1), b)
    return out


def columns_joined(total):
    width = total.shape[1]
    lane = lax.broadcasted_iota(jnp.int32, (8, width), 1)
    left = jnp.where(lane == 0, 0.0, pltpu.roll(total[0:8], 1, 1))
    right = jnp.where(lane == width - 1, 0.0, pltpu.roll(total[16:24], width - 1, 1))
    both = left + total[8:16] + right
    return both[0:4] + both[4:8]


def product(left, right):
    return lax.dot_general(left, right, (((1,), (1,)), ((), ())), preferred_element_type=F32)


def rim_kernel(first_ref, last_ref, s0, s1, s2, s3, fold_ref, core_ref, far_ref, act):
    width, chans = act.shape[0], act.shape[1] // 2
    scale, shift = norm_factors([s0, s1, s2, s3], TILES * 2 * width)
    value = silu(first_ref[0].astype(F32) * scale + shift)
    act[:, pl.ds(0, chans)] = value.astype(BF16)
    value = silu(last_ref[last_ref.shape[0] - 1].astype(F32) * scale + shift)
    act[:, pl.ds(chans, chans)] = value.astype(BF16)
    none = jnp.zeros((24, chans), BF16)
    before = jnp.concatenate([fold_ref[0:24, :chans], none], axis=1)
    after = jnp.concatenate([none, fold_ref[72:96, chans:]], axis=1)
    ends = product(jnp.concatenate([before, after], axis=0), act[...])
    far_ref[...] = columns_joined(ends[0:24])
    core_ref[...] = columns_joined(ends[24:48])


def rim_call(first, last, stats, fold):
    width, chans = first.shape[1:]
    part = jax.ShapeDtypeStruct((4, width), F32)
    return pl.pallas_call(
        rim_kernel,
        out_shape=(part, part),
        in_specs=[VM] * 7,
        out_specs=(VM, VM),
        scratch_shapes=[pltpu.VMEM((width, 2 * chans), BF16)],
        compiler_params=limit(8),
        name="rim",
    )(first, last, *stats, fold)


def taps_kernel(
    x_ref, first_ref, last_ref, s0, s1, s2, s3, fold_ref, head_ref, state_ref, noise_ref, index_ref, out_ref, *rest
):
    rows, width, chans = x_ref.shape
    outs = state_ref.shape[0]
    half = rows // 2
    acts, taps, net = rest[:half], rest[half], rest[half + 1]
    even = (lax.axis_index("tile") & 1) == 0
    scale, shift = norm_factors([s0, s1, s2, s3], rows * width)
    head = head_ref[...].astype(F32)
    head = jnp.concatenate([head, jnp.zeros_like(head)], axis=0)
    none = jnp.zeros_like(head)
    head = jnp.concatenate(
        [jnp.concatenate([head, none], axis=1), jnp.concatenate([none, head], axis=1)], axis=0
    ).astype(BF16)
    direct = []
    for pair in range(half):
        features = jnp.concatenate([x_ref[2 * pair], x_ref[2 * pair + 1]], axis=1)
        direct.append(product(head, features))
        for side in range(2):
            row = 2 * pair + side
            value = first_ref[row] if row < 2 else last_ref[row - 2]
            value = silu(value.astype(F32) * scale + shift)
            acts[pair][:, pl.ds(side * chans, chans)] = value.astype(BF16)
        taps[pair] = product(fold_ref[...], acts[pair][...])
    for r in range(rows):
        pair, side = r // 2, r % 2
        total = taps[pair, 24 + 24 * side : 48 + 24 * side]
        if side == 0 and pair > 0:
            total = total + taps[pair - 1, 72:96]
        if side == 1 and pair + 1 < half:
            total = total + taps[pair + 1, 0:24]
        both = columns_joined(total) + direct[pair][8 * side : 8 * side + 4]
        for o in range(outs):
            net[o, pl.ds(jnp.where(even, r, rows - 1 - r), 1), :] = both[o : o + 1]
    keep, stir, push = step_factors(index_ref[0])
    for t in range(width // 128):
        at = pl.ds(t * 128, 128)
        for o in range(outs):
            direct = keep * state_ref[o, :, at] + stir * noise_ref[o, :, at]
            out_ref[o, :, at] = direct + push * net[o, :, at]


def taps_call(xt, first, last, stats, fold, head, state, noise, index):
    rows, width, chans = xt.shape
    half = rows // 2
    return pl.pallas_call(
        taps_kernel,
        out_shape=jax.ShapeDtypeStruct(state.shape, F32),
        in_specs=[VM] * 11 + [SM],
        out_specs=VM,
        scratch_shapes=[pltpu.VMEM((width, 2 * chans), BF16)] * half
        + [pltpu.VMEM((half, 96, width), F32), pltpu.VMEM(state.shape, F32)],
        compiler_params=limit(24),
        cost_estimate=pl.CostEstimate(
            flops=6144 * width * chans * half, bytes_accessed=1 << 22, transcendentals=2 * xt.size
        ),
        name="taps",
    )(xt, first, last, *stats, fold, head, state, noise, index)


def step_kernel(part_ref, core_ref, far_ref, index_ref, next_ref, blocks_ref):
    outs, rows, width = part_ref.shape
    even = (lax.axis_index("tile") & 1) == 0
    push = step_factors(index_ref[0])[2]
    quarter = width // 512
    line = lax.broadcasted_iota(jnp.int32, (rows, 128), 0)
    at_far = line == jnp.where(even, 0, rows - 1)
    at_core = line == jnp.where(even, rows - 1, 0)
    slot = lax.broadcasted_iota(jnp.int32, (rows, 128), 1) // 32
    for t in range(quarter):
        for o in range(outs):
            values = []
            for k in range(4):
                at = pl.ds((quarter * k + t) * 128, 128)
                extra = jnp.where(at_far, far_ref[o : o + 1, at], 0.0)
                extra = jnp.where(at_core, core_ref[o : o + 1, at], extra)
                values.append(part_ref[o, :, at] + push * extra)
                next_ref[o, :, at] = values[-1]
            for j, mixed in enumerate(turn_quarters(values, slot)):
                blocks_ref[4 * t + j, o] = mixed


def step_call(part, core, far, index):
    outs, rows, width = part.shape
    return pl.pallas_call(
        step_kernel,
        out_shape=(
            jax.ShapeDtypeStruct(part.shape, F32),
            jax.ShapeDtypeStruct((width // 128, outs, rows, 128), F32),
        ),
        in_specs=[VM] * 3 + [SM],
        out_specs=(VM, VM),
        compiler_params=limit(8),
        name="step",
    )(part, core, far, index)


def sums_kernel(got_ref, reg_ref, out_ref):
    count = got_ref.shape[0]
    shape = got_ref.shape[2:]
    own = lax.broadcasted_iota(jnp.int32, shape, 1) // 32 == lax.axis_index("member") // count
    for o in range(got_ref.shape[1]):
        first = got_ref[0, o]
        second = first * first
        for m in range(1, count):
            value = got_ref[m, o]
            first = first + value
            second = second + value * value
        out_ref[0, o] = first
        out_ref[1, o] = second
        out_ref[2, o] = jnp.where(own, reg_ref[o], 0.0)


def sums_call(got, reg):
    return pl.pallas_call(
        sums_kernel,
        out_shape=jax.ShapeDtypeStruct((3,) + got.shape[1:], F32),
        in_specs=[VM, VM],
        out_specs=VM,
        compiler_params=limit(8),
        name="sums",
    )(got, reg)


def spread_kernel(members, one_ref, two_ref, target_ref, out_ref):
    copies, _, outs = out_ref.shape[:3]
    for o in range(outs):
        mean = (one_ref[0, o] + two_ref[0, o]) / members
        var = (one_ref[1, o] + two_ref[1, o]) / members - mean * mean
        scale = jnp.sqrt(1.0 + target_ref[o] / (var + 1.0))
        offset = one_ref[2, o] + two_ref[2, o] + mean - mean * scale
        for k in range(copies):
            out_ref[k, 0, o] = scale
            out_ref[k, 1, o] = offset


def spread_call(one, two, target, copies, members):
    return pl.pallas_call(
        functools.partial(spread_kernel, members),
        out_shape=jax.ShapeDtypeStruct((copies, 2) + one.shape[1:], F32),
        in_specs=[VM, VM, SM],
        out_specs=VM,
        compiler_params=limit(8),
        name="spread",
    )(one, two, target)


def field_kernel(blocks_ref, got_ref, out_ref):
    outs, rows, width = out_ref.shape
    quarter = width // 512
    slot = lax.broadcasted_iota(jnp.int32, (rows, 128), 1) // 32
    for t in range(quarter):
        for o in range(outs):
            values = [
                blocks_ref[4 * t + j, o] * got_ref[4 * t + j, 0, o] + got_ref[4 * t + j, 1, o] for j in range(4)
            ]
            for k, mixed in enumerate(turn_quarters(values, slot)):
                out_ref[o, :, pl.ds((quarter * k + t) * 128, 128)] = mixed


def field_call(blocks, got, shape):
    return pl.pallas_call(
        field_kernel,
        out_shape=jax.ShapeDtypeStruct(shape, F32),
        in_specs=[VM, VM],
        out_specs=VM,
        compiler_params=limit(8),
        name="field",
    )(blocks, got)


def swap(value, bits):
    return lax.ppermute(value, "tile", [(i, i ^ bits) for i in range(TILES)])


def far_swap(value):
    return lax.ppermute(value, "tile", [(1, 2), (2, 1)])


def spread_stats(stats):
    return [stats] + [swap(stats, bits) for bits in (1, 2, 3)]


def shards(
    features, residual_state, noise, regression_mean, step_index, conv_first, conv_second, head_weight, spread_target
):
    member = pltpu.with_memory_space_constraint(features[0], pltpu.HBM)
    xt, core, far, stats = features_call(member, 256)
    stats = spread_stats(stats)
    core, far = swap(core, 1), far_swap(far)
    wt, fold = weights_call(conv_first, conv_second, head_weight)
    last, sums, acts = inner_call(xt, core, stats, wt, 1024)
    first, stats = outer_call(acts, far, stats, sums, wt, 1024)
    stats = spread_stats(stats)
    core, far = rim_call(first, last, stats, fold)
    core, far = swap(core, 1), far_swap(far)
    part = taps_call(
        xt, first, last, stats, fold, head_weight, residual_state[0], noise[0], step_index
    )
    advanced, blocks = step_call(part, core, far, step_index)
    members = lax.axis_size("member")
    size = blocks.shape[0]
    runs = [list(range(i, i + size)) for i in range(0, members, size)]
    got = lax.all_to_all(blocks, "member", 0, 0, tiled=True, axis_index_groups=runs)
    reg = jnp.tile(regression_mean, (1, 1, 4))
    sums = sums_call(got, reg)
    sums = sums + lax.ppermute(sums, "member", [(i, i ^ size) for i in range(members)])
    other = lax.ppermute(sums, "member", [(i, i ^ (3 * size)) for i in range(members)])
    sent = spread_call(sums, other, spread_target, size, members)
    got = lax.all_to_all(sent, "member", 0, 0, tiled=True, axis_index_groups=runs)
    field = field_call(blocks, got, advanced.shape)
    return (field[None], advanced[None])


def solution(mesh):
    cells = P("member", None, "tile", None)
    return jax.shard_map(
        shards,
        mesh=mesh,
        in_specs=(cells, cells, cells, P(None, "tile", "member"), P(), P(), P(), P(), P()),
        out_specs=(cells, cells),
        check_vma=False,
    )
```

```python
import functools

import jax
import jax.numpy as jnp
from jax import lax
from jax.experimental import pallas as pl
from jax.experimental.pallas import tpu as pltpu
from jax.sharding import PartitionSpec as P

GROUP = 4
TILES = 4
F32, BF16 = jnp.float32, jnp.bfloat16
VM = pl.BlockSpec(memory_space=pltpu.VMEM)
SM = pl.BlockSpec(memory_space=pltpu.SMEM)


def limit(mib):
    return pltpu.CompilerParams(vmem_limit_bytes=mib * 1024 * 1024)


def group_total(row):
    lane = lax.broadcasted_iota(jnp.int32, row.shape, 1)
    size = row.shape[1]
    for step in (1, 2):
        up = pltpu.roll(row, step, 1)
        down = pltpu.roll(row, size - step, 1)
        row = row + jnp.where((lane & step) == 0, down, up)
    return row


def merged(parts, count):
    means = [p[0:1, :] for p in parts]
    devs = [p[1:2, :] for p in parts]
    members = len(parts) * GROUP
    mean = group_total(functools.reduce(jnp.add, means)) / members
    spread = functools.reduce(jnp.add, [(m - mean) * (m - mean) for m in means])
    total = group_total(functools.reduce(jnp.add, devs) + count * spread)
    return mean, lax.rsqrt(total / (members * count) + 1e-05)


def silu(values):
    half = 0.5 * values
    return half + half * jnp.tanh(half)


def row_sum(values):
    return values.reshape(-1, 8, values.shape[1]).sum(0)


def write_stats(st_ref, pivot, first, second, count):
    one = jnp.sum(first, axis=0, keepdims=True)
    two = jnp.sum(second, axis=0, keepdims=True)
    mean = pivot + one / count
    dev = two - one * one / count
    pad = jnp.zeros((6, mean.shape[1]), F32)
    st_ref[...] = jnp.concatenate([mean, dev, pad], axis=0)


def features_kernel(x_ref, xt_ref, core_ref, far_ref, st_ref, held, scr, sems):
    rows, full, chans = xt_ref.shape
    pieces, _, _, width = held.shape
    even = (lax.axis_index("tile") & 1) == 0

    def piece(i):
        at = pl.ds(pl.multiple_of(i * width, width), width)
        return pltpu.make_async_copy(x_ref.at[:, :, at], held.at[i], sems.at[i])

    for i in range(pieces):
        piece(i).start()

    def work(i, carry):
        pivot, one, two = carry
        piece(i).wait()
        for part in range(width // 128):
            at = pl.ds(pl.multiple_of(i * width + 128 * part, 128), 128)
            scr[part] = held[i, :, :, pl.ds(128 * part, 128)].astype(F32).reshape(chans * rows, 128)
            for r in range(rows):
                turned = scr[part, pl.ds(r, chans, stride=rows), :].T
                if part == 0 and r == 0:
                    pivot = jnp.where(i == 0, jnp.mean(turned, axis=0, keepdims=True), pivot)
                off = turned - pivot
                one = one + row_sum(off)
                two = two + row_sum(off * off)
                turned = turned.astype(BF16)
                xt_ref[jnp.where(even, r, rows - 1 - r), at] = turned
                if r == 0:
                    top = turned
            core_ref[at] = jnp.where(even, turned, top)
            far_ref[at] = jnp.where(even, top, turned)
        return pivot, one, two

    zero = jnp.zeros((8, chans), F32)
    pivot, one, two = lax.fori_loop(0, pieces, work, (zero[0:1], zero, zero))
    write_stats(st_ref, pivot, one, two, rows * full)


def features_call(x, block):
    chans, rows, width = x.shape
    edge = jax.ShapeDtypeStruct((width, chans), BF16)
    return pl.pallas_call(
        features_kernel,
        out_shape=(
            jax.ShapeDtypeStruct((rows, width, chans), BF16),
            edge,
            edge,
            jax.ShapeDtypeStruct((8, chans), F32),
        ),
        in_specs=[pl.BlockSpec(memory_space=pl.ANY)],
        out_specs=(VM,) * 4,
        scratch_shapes=[
            pltpu.VMEM((width // block, chans, rows, block), BF16),
            pltpu.VMEM((block // 128, chans * rows, 128), F32),
            pltpu.SemaphoreType.DMA((width // block,)),
        ],
        compiler_params=limit(16),
        name="features",
    )(x)


def step_factors(index):
    lane = lax.broadcasted_iota(jnp.int32, (8, 128), 1)
    steps = lane.astype(F32)
    upper = 800.0 ** (1.0 / 7.0)
    lower = 0.002 ** (1.0 / 7.0)
    root = upper + steps / 17.0 * (lower - upper)
    square = root * root
    sigmas = square * square * square * root
    sigma = jnp.sum(jnp.where(lane == index, sigmas, 0.0), axis=1, keepdims=True)
    follow = jnp.sum(jnp.where(lane == index + 1, sigmas, 0.0), axis=1, keepdims=True)
    sigma, follow = jnp.broadcast_to(sigma, lane.shape), jnp.broadcast_to(follow, lane.shape)
    hat = 1.25 * sigma
    spread = hat * hat + 0.25
    skip = 0.25 / spread
    gain = 0.5 * hat / jnp.sqrt(spread)
    rate = (follow - hat) / hat
    keep = 1.0 + rate - rate * skip
    return keep, keep * jnp.sqrt(hat * hat - sigma * sigma), -rate * gain


def place(even, tap):
    return jnp.where(even, tap, 3 * (2 - tap // 3) + tap % 3)


def weights_kernel(first_ref, second_ref, head_ref, wt_ref, fold_ref):
    chans = first_ref.shape[1]
    even = (lax.axis_index("tile") & 1) == 0
    wt_ref[...] = jnp.zeros(wt_ref.shape, BF16)
    for tap in range(9):
        turned = first_ref[place(even, tap)].astype(F32).T.astype(BF16)
        for q in range(2):
            row, col = tap // 3 + q, tap % 3
            wt_ref[pl.ds((3 * row + col) * chans, chans), pl.ds(q * chans, chans)] = turned
    head = jnp.concatenate([head_ref[...].astype(F32)] * 2, axis=0).astype(BF16)
    low = lax.broadcasted_iota(jnp.int32, (8, chans), 0) >= 4
    lines = []
    for row in range(3):
        parts = []
        for col in range(3):
            tap = second_ref[place(even, 3 * row + col)]
            folded = jnp.dot(head, tap, preferred_element_type=F32)
            high = folded.astype(BF16).astype(F32)
            parts.append(jnp.where(low, folded - high, high))
        lines.append(jnp.concatenate(parts, axis=0))
    none = jnp.zeros_like(lines[0])
    left = jnp.concatenate([lines[2], lines[1], lines[0], none], axis=0)
    right = jnp.concatenate([none, lines[2], lines[1], lines[0]], axis=0)
    fold_ref[...] = jnp.concatenate([left, right], axis=1).astype(BF16)


def weights_call(first, second, head):
    chans = first.shape[1]
    return pl.pallas_call(
        weights_kernel,
        out_shape=(
            jax.ShapeDtypeStruct((12 * chans, 2 * chans), BF16),
            jax.ShapeDtypeStruct((96, 2 * chans), BF16),
        ),
        in_specs=[VM] * 3,
        out_specs=(VM, VM),
        compiler_params=limit(16),
        cost_estimate=pl.CostEstimate(flops=1 << 22, bytes_accessed=1 << 21, transcendentals=0),
        name="weights",
    )(first, second, head)


def norm_factors(refs, count):
    mean, scale = merged([ref[...] for ref in refs], count)
    return scale, -mean * scale


def fill(act, buf, value, at, size):
    buf[pl.ds(at + 8, size), :] = value
    act[1, pl.ds(at, size), :] = value.astype(BF16)


def fill_sides(act, buf, at, size):
    act[0, pl.ds(at, size), :] = buf[pl.ds(at + 7, size), :].astype(BF16)
    act[2, pl.ds(at, size), :] = buf[pl.ds(at + 9, size), :].astype(BF16)


def clear_ends(buf):
    size, chans = buf.shape
    buf[pl.ds(0, 8), :] = jnp.zeros((8, chans), F32)
    buf[pl.ds(size - 8, 8), :] = jnp.zeros((8, chans), F32)


def two_rows(acts, wt_ref, at, block):
    left = jnp.concatenate([act[s, pl.ds(at, block), :] for act in acts for s in range(3)], axis=1)
    out = jnp.dot(left, wt_ref[...], preferred_element_type=F32)
    chans = out.shape[1] // 2
    return out[:, :chans], out[:, chans:]


def join(acts, wt_ref, hid_ref, lines, block, late, fresh, carry):
    width = hid_ref.shape[1]
    pivot, one, two = carry
    for at in range(0, width, block):
        a, b = two_rows(acts, wt_ref, at, block)
        if at == 0:
            for act, buf, read in late:
                rest = width - block - 16
                fill(act, buf, read(block + 16, rest), block + 16, rest)
                fill_sides(act, buf, block, width - block)
        if not late or at > 0:
            start = 0 if late else at
            size = at + block - start
            for act, buf, read in fresh:
                fill(act, buf, read(start, size), start, size)
                if start > 0:
                    fill_sides(act, buf, start - block, block)
        hid_ref[lines[0], pl.ds(at, block), :] = a.astype(BF16)
        hid_ref[lines[1], pl.ds(at, block), :] = b.astype(BF16)
        if pivot is None:
            pivot = jnp.mean(a[0:8], axis=0, keepdims=True)
        a, b = a - pivot, b - pivot
        one = one + row_sum(a + b)
        two = two + row_sum(a * a + b * b)
    for act, buf, read in fresh:
        start = 0 if late else width - block
        fill_sides(act, buf, start, width - start)
    return pivot, one, two


def inner_kernel(block, x_ref, core_ref, s0, s1, s2, s3, wt_ref, hid_ref, sum_ref, *rest):
    rows, width, chans = x_ref.shape
    acts, bufs = rest[: rows + 1], rest[rows + 1 :]
    scale, shift = norm_factors([s0, s1, s2, s3], rows * width)
    for buf in bufs:
        clear_ends(buf)

    def line(row):
        def read(at, size):
            span = pl.ds(at, size)
            value = core_ref[span, :] if row == rows else x_ref[row, span, :]
            return silu(value.astype(F32) * scale + shift)

        return acts[row], bufs[row % len(bufs)], read

    early = [line(row) for row in range(1, 5)]
    for act, buf, read in early:
        fill(act, buf, read(0, block + 16), 0, block + 16)
        fill_sides(act, buf, 0, block)
    zero = jnp.zeros((8, chans), F32)
    carry = (None, zero, zero)
    for pair, fresh in ((0, (5, 6)), (1, (7, 8)), (2, (0,))):
        group = acts[2 * pair + 1 : 2 * pair + 5]
        lines = (2 * pair, 2 * pair + 1)
        fresh = [line(row) for row in fresh]
        carry = join(group, wt_ref, hid_ref, lines, block, early if pair == 0 else [], fresh, carry)
    pivot, one, two = carry
    sum_ref[0] = jnp.broadcast_to(pivot, one.shape)
    sum_ref[1] = one
    sum_ref[2] = two


def inner_call(xt, core, stats, wt, block):
    rows, width, chans = xt.shape
    act = jax.ShapeDtypeStruct((3, width, chans), BF16)
    hid, sums, *acts = pl.pallas_call(
        functools.partial(inner_kernel, block),
        out_shape=(
            jax.ShapeDtypeStruct((rows - 2, width, chans), BF16),
            jax.ShapeDtypeStruct((3, 8, chans), F32),
            act,
            act,
            act,
        ),
        in_specs=[VM] * 7,
        out_specs=(VM,) * 5,
        scratch_shapes=[pltpu.VMEM(act.shape, BF16)] * (rows - 2)
        + [pltpu.VMEM((width + 16, chans), F32)] * 4,
        compiler_params=limit(32),
        cost_estimate=pl.CostEstimate(
            flops=24 * rows * width * chans * chans, bytes_accessed=1 << 22, transcendentals=xt.size
        ),
        name="inner",
    )(xt, core, *stats, wt)
    return hid, sums, acts


def outer_kernel(block, far_ref, a0, a1, a2, s0, s1, s2, s3, sum_ref, wt_ref, hid_ref, st_ref, act, buf):
    width, chans = far_ref.shape
    tile = lax.axis_index("tile")
    linked = ((tile == 1) | (tile == 2)).astype(F32)
    count = TILES * 2 * width
    scale, shift = norm_factors([s0, s1, s2, s3], count)
    clear_ends(buf)

    def read(at, size):
        return silu(far_ref[pl.ds(at, size), :].astype(F32) * scale + shift) * linked

    fill(act, buf, read(0, block + 16), 0, block + 16)
    fill_sides(act, buf, 0, block)
    carry = (sum_ref[0, 0:1], sum_ref[1], sum_ref[2])
    early = [(act, buf, read)]
    pivot, one, two = join([act, a0, a1, a2], wt_ref, hid_ref, (0, 1), block, early, [], carry)
    write_stats(st_ref, pivot, one, two, count)


def outer_call(acts, far, stats, sums, wt, block):
    width, chans = far.shape
    return pl.pallas_call(
        functools.partial(outer_kernel, block),
        out_shape=(
            jax.ShapeDtypeStruct((2, width, chans), BF16),
            jax.ShapeDtypeStruct((8, chans), F32),
        ),
        in_specs=[VM] * 10,
        out_specs=(VM,) * 2,
        scratch_shapes=[pltpu.VMEM((3, width, chans), BF16), pltpu.VMEM((width + 16, chans), F32)],
        compiler_params=limit(12),
        name="outer",
    )(far, *acts, *stats, sums, wt)


def turn_quarters(values, slot):
    low, right = slot < 2, (slot & 1) == 0
    halves = []
    for a, b in ((values[0], values[2]), (values[1], values[3])):
        moved = pltpu.roll(jnp.where(low, b, a), 64, 1)
        halves.append((jnp.where(low, a, moved), jnp.where(low, moved, b)))
    out = [None] * 4
    for k in range(2):
        a, b = halves[0][k], halves[1][k]
        out[2 * k] = jnp.where(right, a, pltpu.roll(b, 32, 1))
        out[2 * k + 1] = jnp.where(right, pltpu.roll(a, 96, 1), b)
    return out


def columns_joined(total):
    width = total.shape[1]
    lane = lax.broadcasted_iota(jnp.int32, (8, width), 1)
    left = jnp.where(lane == 0, 0.0, pltpu.roll(total[0:8], 1, 1))
    right = jnp.where(lane == width - 1, 0.0, pltpu.roll(total[16:24], width - 1, 1))
    both = left + total[8:16] + right
    return both[0:4] + both[4:8]


def product(left, right):
    return lax.dot_general(left, right, (((1,), (1,)), ((), ())), preferred_element_type=F32)


def rim_kernel(first_ref, last_ref, s0, s1, s2, s3, fold_ref, core_ref, far_ref, act):
    width, chans = act.shape[0], act.shape[1] // 2
    scale, shift = norm_factors([s0, s1, s2, s3], TILES * 2 * width)
    value = silu(first_ref[0].astype(F32) * scale + shift)
    act[:, pl.ds(0, chans)] = value.astype(BF16)
    value = silu(last_ref[last_ref.shape[0] - 1].astype(F32) * scale + shift)
    act[:, pl.ds(chans, chans)] = value.astype(BF16)
    none = jnp.zeros((24, chans), BF16)
    before = jnp.concatenate([fold_ref[0:24, :chans], none], axis=1)
    after = jnp.concatenate([none, fold_ref[72:96, chans:]], axis=1)
    ends = product(jnp.concatenate([before, after], axis=0), act[...])
    far_ref[...] = columns_joined(ends[0:24])
    core_ref[...] = columns_joined(ends[24:48])


def rim_call(first, last, stats, fold):
    width, chans = first.shape[1:]
    part = jax.ShapeDtypeStruct((4, width), F32)
    return pl.pallas_call(
        rim_kernel,
        out_shape=(part, part),
        in_specs=[VM] * 7,
        out_specs=(VM, VM),
        scratch_shapes=[pltpu.VMEM((width, 2 * chans), BF16)],
        compiler_params=limit(8),
        name="rim",
    )(first, last, *stats, fold)


def taps_kernel(
    x_ref, first_ref, last_ref, s0, s1, s2, s3, fold_ref, head_ref, state_ref, noise_ref, index_ref, out_ref, *rest
):
    rows, width, chans = x_ref.shape
    outs = state_ref.shape[0]
    half = rows // 2
    acts, taps, net = rest[:half], rest[half], rest[half + 1]
    even = (lax.axis_index("tile") & 1) == 0
    scale, shift = norm_factors([s0, s1, s2, s3], rows * width)
    head = head_ref[...].astype(F32)
    head = jnp.concatenate([head, jnp.zeros_like(head)], axis=0)
    none = jnp.zeros_like(head)
    head = jnp.concatenate(
        [jnp.concatenate([head, none], axis=1), jnp.concatenate([none, head], axis=1)], axis=0
    ).astype(BF16)
    direct = []
    for pair in range(half):
        features = jnp.concatenate([x_ref[2 * pair], x_ref[2 * pair + 1]], axis=1)
        direct.append(product(head, features))
        for side in range(2):
            row = 2 * pair + side
            value = first_ref[row] if row < 2 else last_ref[row - 2]
            value = silu(value.astype(F32) * scale + shift)
            acts[pair][:, pl.ds(side * chans, chans)] = value.astype(BF16)
        taps[pair] = product(fold_ref[...], acts[pair][...])
    for r in range(rows):
        pair, side = r // 2, r % 2
        total = taps[pair, 24 + 24 * side : 48 + 24 * side]
        if side == 0 and pair > 0:
            total = total + taps[pair - 1, 72:96]
        if side == 1 and pair + 1 < half:
            total = total + taps[pair + 1, 0:24]
        both = columns_joined(total) + direct[pair][8 * side : 8 * side + 4]
        for o in range(outs):
            net[o, pl.ds(jnp.where(even, r, rows - 1 - r), 1), :] = both[o : o + 1]
    keep, stir, push = step_factors(index_ref[0])
    for t in range(width // 128):
        at = pl.ds(t * 128, 128)
        for o in range(outs):
            direct = keep * state_ref[o, :, at] + stir * noise_ref[o, :, at]
            out_ref[o, :, at] = direct + push * net[o, :, at]


def taps_call(xt, first, last, stats, fold, head, state, noise, index):
    rows, width, chans = xt.shape
    half = rows // 2
    return pl.pallas_call(
        taps_kernel,
        out_shape=jax.ShapeDtypeStruct(state.shape, F32),
        in_specs=[VM] * 11 + [SM],
        out_specs=VM,
        scratch_shapes=[pltpu.VMEM((width, 2 * chans), BF16)] * half
        + [pltpu.VMEM((half, 96, width), F32), pltpu.VMEM(state.shape, F32)],
        compiler_params=limit(24),
        cost_estimate=pl.CostEstimate(
            flops=6144 * width * chans * half, bytes_accessed=1 << 22, transcendentals=2 * xt.size
        ),
        name="taps",
    )(xt, first, last, *stats, fold, head, state, noise, index)


def step_kernel(part_ref, core_ref, far_ref, index_ref, next_ref, blocks_ref, kept_ref):
    outs, rows, width = part_ref.shape
    even = (lax.axis_index("tile") & 1) == 0
    push = step_factors(index_ref[0])[2]
    quarter = width // 512
    line = lax.broadcasted_iota(jnp.int32, (rows, 128), 0)
    at_far = line == jnp.where(even, 0, rows - 1)
    at_core = line == jnp.where(even, rows - 1, 0)
    slot = lax.broadcasted_iota(jnp.int32, (rows, 128), 1) // 32
    for t in range(quarter):
        for o in range(outs):
            values = []
            for k in range(4):
                at = pl.ds((quarter * k + t) * 128, 128)
                extra = jnp.where(at_far, far_ref[o : o + 1, at], 0.0)
                extra = jnp.where(at_core, core_ref[o : o + 1, at], extra)
                values.append(part_ref[o, :, at] + push * extra)
                next_ref[o, :, at] = values[-1]
            for j, mixed in enumerate(turn_quarters(values, slot)):
                blocks_ref[4 * t + j, o] = mixed
                kept_ref[4 * t + j, o] = mixed


def step_call(part, core, far, index):
    outs, rows, width = part.shape
    return pl.pallas_call(
        step_kernel,
        out_shape=(
            jax.ShapeDtypeStruct(part.shape, F32),
            jax.ShapeDtypeStruct((width // 128, outs, rows, 128), F32),
            pltpu.VMEM((width // 128, outs, rows, 128), F32),
        ),
        in_specs=[VM] * 3 + [SM],
        out_specs=(VM, VM, VM),
        compiler_params=limit(8),
        name="step",
    )(part, core, far, index)


def sums_kernel(got_ref, reg_ref, out_ref):
    count = got_ref.shape[0]
    shape = got_ref.shape[2:]
    own = lax.broadcasted_iota(jnp.int32, shape, 1) // 32 == lax.axis_index("member") // count
    for o in range(got_ref.shape[1]):
        first = got_ref[0, o]
        second = first * first
        for m in range(1, count):
            value = got_ref[m, o]
            first = first + value
            second = second + value * value
        out_ref[0, o] = first
        out_ref[1, o] = second
        out_ref[2, o] = jnp.where(own, reg_ref[o], 0.0)


def sums_call(got, reg):
    return pl.pallas_call(
        sums_kernel,
        out_shape=jax.ShapeDtypeStruct((3,) + got.shape[1:], F32),
        in_specs=[VM, VM],
        out_specs=VM,
        compiler_params=limit(8),
        name="sums",
    )(got, reg)


def spread_kernel(members, one_ref, two_ref, target_ref, out_ref):
    copies, _, outs = out_ref.shape[:3]
    for o in range(outs):
        mean = (one_ref[0, o] + two_ref[0, o]) / members
        var = (one_ref[1, o] + two_ref[1, o]) / members - mean * mean
        scale = jnp.sqrt(1.0 + target_ref[o] / (var + 1.0))
        offset = one_ref[2, o] + two_ref[2, o] + mean - mean * scale
        for k in range(copies):
            out_ref[k, 0, o] = scale
            out_ref[k, 1, o] = offset


def spread_call(one, two, target, copies, members):
    return pl.pallas_call(
        functools.partial(spread_kernel, members),
        out_shape=jax.ShapeDtypeStruct((copies, 2) + one.shape[1:], F32),
        in_specs=[VM, VM, SM],
        out_specs=VM,
        compiler_params=limit(8),
        name="spread",
    )(one, two, target)


def field_kernel(blocks_ref, got_ref, out_ref):
    outs, rows, width = out_ref.shape
    quarter = width // 512
    slot = lax.broadcasted_iota(jnp.int32, (rows, 128), 1) // 32
    for t in range(quarter):
        for o in range(outs):
            values = [
                blocks_ref[4 * t + j, o] * got_ref[4 * t + j, 0, o] + got_ref[4 * t + j, 1, o] for j in range(4)
            ]
            for k, mixed in enumerate(turn_quarters(values, slot)):
                out_ref[o, :, pl.ds((quarter * k + t) * 128, 128)] = mixed


def field_call(blocks, got, shape):
    return pl.pallas_call(
        field_kernel,
        out_shape=jax.ShapeDtypeStruct(shape, F32),
        in_specs=[VM, VM],
        out_specs=VM,
        compiler_params=limit(8),
        name="field",
    )(blocks, got)


def swap(value, bits):
    return lax.ppermute(value, "tile", [(i, i ^ bits) for i in range(TILES)])


def far_swap(value):
    return lax.ppermute(value, "tile", [(1, 2), (2, 1)])


def spread_stats(stats):
    return [stats] + [swap(stats, bits) for bits in (1, 2, 3)]


def shards(
    features, residual_state, noise, regression_mean, step_index, conv_first, conv_second, head_weight, spread_target
):
    member = pltpu.with_memory_space_constraint(features[0], pltpu.HBM)
    xt, core, far, stats = features_call(member, 512)
    stats = spread_stats(stats)
    core, far = swap(core, 1), far_swap(far)
    wt, fold = weights_call(conv_first, conv_second, head_weight)
    last, sums, acts = inner_call(xt, core, stats, wt, 1024)
    first, stats = outer_call(acts, far, stats, sums, wt, 1024)
    stats = spread_stats(stats)
    core, far = rim_call(first, last, stats, fold)
    core, far = swap(core, 1), far_swap(far)
    part = taps_call(
        xt, first, last, stats, fold, head_weight, residual_state[0], noise[0], step_index
    )
    advanced, blocks, kept = step_call(part, core, far, step_index)
    members = lax.axis_size("member")
    size = blocks.shape[0]
    runs = [list(range(i, i + size)) for i in range(0, members, size)]
    got = lax.all_to_all(blocks, "member", 0, 0, tiled=True, axis_index_groups=runs)
    reg = jnp.tile(regression_mean, (1, 1, 4))
    sums = sums_call(got, reg)
    sums = sums + lax.ppermute(sums, "member", [(i, i ^ size) for i in range(members)])
    other = lax.ppermute(sums, "member", [(i, i ^ (3 * size)) for i in range(members)])
    sent = spread_call(sums, other, spread_target, size, members)
    got = lax.all_to_all(sent, "member", 0, 0, tiled=True, axis_index_groups=runs)
    field = field_call(kept, got, advanced.shape)
    return (field[None], advanced[None])


def solution(mesh):
    cells = P("member", None, "tile", None)
    return jax.shard_map(
        shards,
        mesh=mesh,
        in_specs=(cells, cells, cells, P(None, "tile", "member"), P(), P(), P(), P(), P()),
        out_specs=(cells, cells),
        check_vma=False,
    )
```

```python
import functools

import jax
import jax.numpy as jnp
from jax import lax
from jax.experimental import pallas as pl
from jax.experimental.pallas import tpu as pltpu
from jax.sharding import PartitionSpec as P

GROUP = 4
TILES = 4
F32, BF16 = jnp.float32, jnp.bfloat16
VM = pl.BlockSpec(memory_space=pltpu.VMEM)
SM = pl.BlockSpec(memory_space=pltpu.SMEM)


def limit(mib):
    return pltpu.CompilerParams(vmem_limit_bytes=mib * 1024 * 1024)


def group_total(row):
    lane = lax.broadcasted_iota(jnp.int32, row.shape, 1)
    size = row.shape[1]
    for step in (1, 2):
        up = pltpu.roll(row, step, 1)
        down = pltpu.roll(row, size - step, 1)
        row = row + jnp.where((lane & step) == 0, down, up)
    return row


def merged(parts, count):
    means = [p[0:1, :] for p in parts]
    devs = [p[1:2, :] for p in parts]
    members = len(parts) * GROUP
    mean = group_total(functools.reduce(jnp.add, means)) / members
    spread = functools.reduce(jnp.add, [(m - mean) * (m - mean) for m in means])
    total = group_total(functools.reduce(jnp.add, devs) + count * spread)
    return mean, lax.rsqrt(total / (members * count) + 1e-05)


def silu(values):
    half = 0.5 * values
    return half + half * jnp.tanh(half)


def row_sum(values):
    return values.reshape(-1, 8, values.shape[1]).sum(0)


def write_stats(st_ref, pivot, first, second, count):
    one = jnp.sum(first, axis=0, keepdims=True)
    two = jnp.sum(second, axis=0, keepdims=True)
    mean = pivot + one / count
    dev = two - one * one / count
    pad = jnp.zeros((6, mean.shape[1]), F32)
    st_ref[...] = jnp.concatenate([mean, dev, pad], axis=0)


def features_kernel(x_ref, xt_ref, core_ref, far_ref, st_ref, held, scr, sems):
    rows, full, chans = xt_ref.shape
    pieces, _, _, width = held.shape
    even = (lax.axis_index("tile") & 1) == 0

    def piece(i):
        at = pl.ds(pl.multiple_of(i * width, width), width)
        return pltpu.make_async_copy(x_ref.at[:, :, at], held.at[i], sems.at[i])

    for i in range(pieces):
        piece(i).start()

    def work(i, carry):
        pivot, one, two = carry
        piece(i).wait()
        for part in range(width // 128):
            at = pl.ds(pl.multiple_of(i * width + 128 * part, 128), 128)
            scr[part] = held[i, :, :, pl.ds(128 * part, 128)].astype(F32).reshape(chans * rows, 128)
            for r in range(rows):
                turned = scr[part, pl.ds(r, chans, stride=rows), :].T
                if part == 0 and r == 0:
                    pivot = jnp.where(i == 0, jnp.mean(turned, axis=0, keepdims=True), pivot)
                off = turned - pivot
                one = one + row_sum(off)
                two = two + row_sum(off * off)
                turned = turned.astype(BF16)
                xt_ref[jnp.where(even, r, rows - 1 - r), at] = turned
                if r == 0:
                    top = turned
            core_ref[at] = jnp.where(even, turned, top)
            far_ref[at] = jnp.where(even, top, turned)
        return pivot, one, two

    zero = jnp.zeros((8, chans), F32)
    pivot, one, two = lax.fori_loop(0, pieces, work, (zero[0:1], zero, zero))
    write_stats(st_ref, pivot, one, two, rows * full)


def features_call(x, block):
    chans, rows, width = x.shape
    edge = jax.ShapeDtypeStruct((width, chans), BF16)
    return pl.pallas_call(
        features_kernel,
        out_shape=(
            jax.ShapeDtypeStruct((rows, width, chans), BF16),
            edge,
            edge,
            jax.ShapeDtypeStruct((8, chans), F32),
        ),
        in_specs=[pl.BlockSpec(memory_space=pl.ANY)],
        out_specs=(VM,) * 4,
        scratch_shapes=[
            pltpu.VMEM((width // block, chans, rows, block), BF16),
            pltpu.VMEM((block // 128, chans * rows, 128), F32),
            pltpu.SemaphoreType.DMA((width // block,)),
        ],
        compiler_params=limit(16),
        name="features",
    )(x)


def step_factors(index):
    lane = lax.broadcasted_iota(jnp.int32, (8, 128), 1)
    steps = lane.astype(F32)
    upper = 800.0 ** (1.0 / 7.0)
    lower = 0.002 ** (1.0 / 7.0)
    root = upper + steps / 17.0 * (lower - upper)
    square = root * root
    sigmas = square * square * square * root
    sigma = jnp.sum(jnp.where(lane == index, sigmas, 0.0), axis=1, keepdims=True)
    follow = jnp.sum(jnp.where(lane == index + 1, sigmas, 0.0), axis=1, keepdims=True)
    sigma, follow = jnp.broadcast_to(sigma, lane.shape), jnp.broadcast_to(follow, lane.shape)
    hat = 1.25 * sigma
    spread = hat * hat + 0.25
    skip = 0.25 / spread
    gain = 0.5 * hat / jnp.sqrt(spread)
    rate = (follow - hat) / hat
    keep = 1.0 + rate - rate * skip
    return keep, keep * jnp.sqrt(hat * hat - sigma * sigma), -rate * gain


def place(even, tap):
    return jnp.where(even, tap, 3 * (2 - tap // 3) + tap % 3)


def weights_kernel(first_ref, second_ref, head_ref, wt_ref, fold_ref):
    chans = first_ref.shape[1]
    even = (lax.axis_index("tile") & 1) == 0
    wt_ref[...] = jnp.zeros(wt_ref.shape, BF16)
    for tap in range(9):
        turned = first_ref[place(even, tap)].astype(F32).T.astype(BF16)
        for q in range(2):
            row, col = tap // 3 + q, tap % 3
            wt_ref[pl.ds((3 * row + col) * chans, chans), pl.ds(q * chans, chans)] = turned
    head = jnp.concatenate([head_ref[...].astype(F32)] * 2, axis=0).astype(BF16)
    low = lax.broadcasted_iota(jnp.int32, (8, chans), 0) >= 4
    lines = []
    for row in range(3):
        parts = []
        for col in range(3):
            tap = second_ref[place(even, 3 * row + col)]
            folded = jnp.dot(head, tap, preferred_element_type=F32)
            high = folded.astype(BF16).astype(F32)
            parts.append(jnp.where(low, folded - high, high))
        lines.append(jnp.concatenate(parts, axis=0))
    none = jnp.zeros_like(lines[0])
    left = jnp.concatenate([lines[2], lines[1], lines[0], none], axis=0)
    right = jnp.concatenate([none, lines[2], lines[1], lines[0]], axis=0)
    fold_ref[...] = jnp.concatenate([left, right], axis=1).astype(BF16)


def weights_call(first, second, head):
    chans = first.shape[1]
    return pl.pallas_call(
        weights_kernel,
        out_shape=(
            jax.ShapeDtypeStruct((12 * chans, 2 * chans), BF16),
            jax.ShapeDtypeStruct((96, 2 * chans), BF16),
        ),
        in_specs=[VM] * 3,
        out_specs=(VM, VM),
        compiler_params=limit(16),
        cost_estimate=pl.CostEstimate(flops=1 << 22, bytes_accessed=1 << 21, transcendentals=0),
        name="weights",
    )(first, second, head)


def norm_factors(refs, count):
    mean, scale = merged([ref[...] for ref in refs], count)
    return scale, -mean * scale


def fill(act, buf, value, at, size):
    buf[pl.ds(at + 8, size), :] = value
    act[1, pl.ds(at, size), :] = value.astype(BF16)


def fill_sides(act, buf, at, size):
    act[0, pl.ds(at, size), :] = buf[pl.ds(at + 7, size), :].astype(BF16)
    act[2, pl.ds(at, size), :] = buf[pl.ds(at + 9, size), :].astype(BF16)


def clear_ends(buf):
    size, chans = buf.shape
    buf[pl.ds(0, 8), :] = jnp.zeros((8, chans), F32)
    buf[pl.ds(size - 8, 8), :] = jnp.zeros((8, chans), F32)


def two_rows(acts, wt_ref, at, block):
    left = jnp.concatenate([act[s, pl.ds(at, block), :] for act in acts for s in range(3)], axis=1)
    out = jnp.dot(left, wt_ref[...], preferred_element_type=F32)
    chans = out.shape[1] // 2
    return out[:, :chans], out[:, chans:]


def join(acts, wt_ref, hid_ref, lines, block, late, fresh, carry):
    width = hid_ref.shape[1]
    pivot, one, two = carry
    for at in range(0, width, block):
        a, b = two_rows(acts, wt_ref, at, block)
        if at == 0:
            for act, buf, read in late:
                rest = width - block - 16
                fill(act, buf, read(block + 16, rest), block + 16, rest)
                fill_sides(act, buf, block, width - block)
        if not late or at > 0:
            start = 0 if late else at
            size = at + block - start
            for act, buf, read in fresh:
                fill(act, buf, read(start, size), start, size)
                if start > 0:
                    fill_sides(act, buf, start - block, block)
        hid_ref[lines[0], pl.ds(at, block), :] = a.astype(BF16)
        hid_ref[lines[1], pl.ds(at, block), :] = b.astype(BF16)
        if pivot is None:
            pivot = jnp.mean(a[0:8], axis=0, keepdims=True)
        a, b = a - pivot, b - pivot
        one = one + row_sum(a + b)
        two = two + row_sum(a * a + b * b)
    for act, buf, read in fresh:
        start = 0 if late else width - block
        fill_sides(act, buf, start, width - start)
    return pivot, one, two


def inner_kernel(block, x_ref, core_ref, s0, s1, s2, s3, wt_ref, hid_ref, sum_ref, *rest):
    rows, width, chans = x_ref.shape
    acts, bufs = rest[: rows + 1], rest[rows + 1 :]
    scale, shift = norm_factors([s0, s1, s2, s3], rows * width)
    for buf in bufs:
        clear_ends(buf)

    def line(row):
        def read(at, size):
            span = pl.ds(at, size)
            value = core_ref[span, :] if row == rows else x_ref[row, span, :]
            return silu(value.astype(F32) * scale + shift)

        return acts[row], bufs[row % len(bufs)], read

    early = [line(row) for row in range(1, 5)]
    for act, buf, read in early:
        fill(act, buf, read(0, block + 16), 0, block + 16)
        fill_sides(act, buf, 0, block)
    zero = jnp.zeros((8, chans), F32)
    carry = (None, zero, zero)
    for pair, fresh in ((0, (5, 6)), (1, (7, 8)), (2, (0,))):
        group = acts[2 * pair + 1 : 2 * pair + 5]
        lines = (2 * pair, 2 * pair + 1)
        fresh = [line(row) for row in fresh]
        carry = join(group, wt_ref, hid_ref, lines, block, early if pair == 0 else [], fresh, carry)
    pivot, one, two = carry
    sum_ref[0] = jnp.broadcast_to(pivot, one.shape)
    sum_ref[1] = one
    sum_ref[2] = two


def inner_call(xt, core, stats, wt, block):
    rows, width, chans = xt.shape
    act = jax.ShapeDtypeStruct((3, width, chans), BF16)
    hid, sums, *acts = pl.pallas_call(
        functools.partial(inner_kernel, block),
        out_shape=(
            jax.ShapeDtypeStruct((rows - 2, width, chans), BF16),
            jax.ShapeDtypeStruct((3, 8, chans), F32),
            act,
            act,
            act,
        ),
        in_specs=[VM] * 7,
        out_specs=(VM,) * 5,
        scratch_shapes=[pltpu.VMEM(act.shape, BF16)] * (rows - 2)
        + [pltpu.VMEM((width + 16, chans), F32)] * 4,
        compiler_params=limit(32),
        cost_estimate=pl.CostEstimate(
            flops=24 * rows * width * chans * chans, bytes_accessed=1 << 22, transcendentals=xt.size
        ),
        name="inner",
    )(xt, core, *stats, wt)
    return hid, sums, acts


def outer_kernel(block, far_ref, a0, a1, a2, s0, s1, s2, s3, sum_ref, wt_ref, hid_ref, st_ref, act, buf):
    width, chans = far_ref.shape
    tile = lax.axis_index("tile")
    linked = ((tile == 1) | (tile == 2)).astype(F32)
    count = TILES * 2 * width
    scale, shift = norm_factors([s0, s1, s2, s3], count)
    clear_ends(buf)

    def read(at, size):
        return silu(far_ref[pl.ds(at, size), :].astype(F32) * scale + shift) * linked

    fill(act, buf, read(0, block + 16), 0, block + 16)
    fill_sides(act, buf, 0, block)
    carry = (sum_ref[0, 0:1], sum_ref[1], sum_ref[2])
    early = [(act, buf, read)]
    pivot, one, two = join([act, a0, a1, a2], wt_ref, hid_ref, (0, 1), block, early, [], carry)
    write_stats(st_ref, pivot, one, two, count)


def outer_call(acts, far, stats, sums, wt, block):
    width, chans = far.shape
    return pl.pallas_call(
        functools.partial(outer_kernel, block),
        out_shape=(
            jax.ShapeDtypeStruct((2, width, chans), BF16),
            jax.ShapeDtypeStruct((8, chans), F32),
        ),
        in_specs=[VM] * 10,
        out_specs=(VM,) * 2,
        scratch_shapes=[pltpu.VMEM((3, width, chans), BF16), pltpu.VMEM((width + 16, chans), F32)],
        compiler_params=limit(12),
        name="outer",
    )(far, *acts, *stats, sums, wt)


def turn_quarters(values, slot):
    low, right = slot < 2, (slot & 1) == 0
    halves = []
    for a, b in ((values[0], values[2]), (values[1], values[3])):
        moved = pltpu.roll(jnp.where(low, b, a), 64, 1)
        halves.append((jnp.where(low, a, moved), jnp.where(low, moved, b)))
    out = [None] * 4
    for k in range(2):
        a, b = halves[0][k], halves[1][k]
        out[2 * k] = jnp.where(right, a, pltpu.roll(b, 32, 1))
        out[2 * k + 1] = jnp.where(right, pltpu.roll(a, 96, 1), b)
    return out


def columns_joined(total):
    width = total.shape[1]
    lane = lax.broadcasted_iota(jnp.int32, (8, width), 1)
    left = jnp.where(lane == 0, 0.0, pltpu.roll(total[0:8], 1, 1))
    right = jnp.where(lane == width - 1, 0.0, pltpu.roll(total[16:24], width - 1, 1))
    both = left + total[8:16] + right
    return both[0:4] + both[4:8]


def product(left, right):
    return lax.dot_general(left, right, (((1,), (1,)), ((), ())), preferred_element_type=F32)


def rim_kernel(first_ref, last_ref, s0, s1, s2, s3, fold_ref, core_ref, far_ref, top_ref, bottom_ref):
    width, chans = top_ref.shape
    scale, shift = norm_factors([s0, s1, s2, s3], TILES * 2 * width)
    value = silu(first_ref[0].astype(F32) * scale + shift)
    top_ref[...] = value.astype(BF16)
    value = silu(last_ref[last_ref.shape[0] - 1].astype(F32) * scale + shift)
    bottom_ref[...] = value.astype(BF16)
    none = jnp.zeros((24, chans), BF16)
    before = jnp.concatenate([fold_ref[0:24, :chans], none], axis=1)
    after = jnp.concatenate([none, fold_ref[72:96, chans:]], axis=1)
    both = jnp.concatenate([top_ref[...], bottom_ref[...]], axis=1)
    ends = product(jnp.concatenate([before, after], axis=0), both)
    far_ref[...] = columns_joined(ends[0:24])
    core_ref[...] = columns_joined(ends[24:48])


def rim_call(first, last, stats, fold):
    width, chans = first.shape[1:]
    part = jax.ShapeDtypeStruct((4, width), F32)
    act = jax.ShapeDtypeStruct((width, chans), BF16)
    return pl.pallas_call(
        rim_kernel,
        out_shape=(part, part, act, act),
        in_specs=[VM] * 7,
        out_specs=(VM,) * 4,
        compiler_params=limit(8),
        name="rim",
    )(first, last, *stats, fold)


def base_kernel(x_ref, head_ref, state_ref, noise_ref, index_ref, out_ref, net):
    rows, width, _ = x_ref.shape
    outs = state_ref.shape[0]
    even = (lax.axis_index("tile") & 1) == 0
    head = head_ref[...].astype(F32)
    head = jnp.concatenate([head, jnp.zeros_like(head)], axis=0)
    none = jnp.zeros_like(head)
    head = jnp.concatenate(
        [jnp.concatenate([head, none], axis=1), jnp.concatenate([none, head], axis=1)], axis=0
    ).astype(BF16)
    for pair in range(rows // 2):
        features = jnp.concatenate([x_ref[2 * pair], x_ref[2 * pair + 1]], axis=1)
        both = product(head, features)
        for side in range(2):
            r = 2 * pair + side
            for o in range(outs):
                line = both[8 * side + o : 8 * side + o + 1]
                net[o, pl.ds(jnp.where(even, r, rows - 1 - r), 1), :] = line
    keep, stir, push = step_factors(index_ref[0])
    for t in range(width // 128):
        at = pl.ds(t * 128, 128)
        for o in range(outs):
            direct = keep * state_ref[o, :, at] + stir * noise_ref[o, :, at]
            out_ref[o, :, at] = direct + push * net[o, :, at]


def base_call(xt, head, state, noise, index):
    return pl.pallas_call(
        base_kernel,
        out_shape=jax.ShapeDtypeStruct(state.shape, F32),
        in_specs=[VM] * 4 + [SM],
        out_specs=VM,
        scratch_shapes=[pltpu.VMEM(state.shape, F32)],
        compiler_params=limit(12),
        cost_estimate=pl.CostEstimate(flops=1 << 24, bytes_accessed=1 << 20, transcendentals=0),
        name="base",
    )(xt, head, state, noise, index)


def taps_kernel(first_ref, last_ref, top_ref, bottom_ref, s0, s1, s2, s3, fold_ref, base_ref, index_ref, out_ref, *rest):
    outs, rows, width = base_ref.shape
    half = rows // 2
    acts, taps, net = rest[: rows - 2], rest[rows - 2], rest[rows - 1]
    acts = (top_ref,) + acts + (bottom_ref,)
    even = (lax.axis_index("tile") & 1) == 0
    scale, shift = norm_factors([s0, s1, s2, s3], rows * width)
    for pair in range(half):
        for row in (2 * pair, 2 * pair + 1):
            if 0 < row < rows - 1:
                value = first_ref[row] if row < 2 else last_ref[row - 2]
                acts[row][...] = silu(value.astype(F32) * scale + shift).astype(BF16)
        both = jnp.concatenate([acts[2 * pair][...], acts[2 * pair + 1][...]], axis=1)
        taps[pair] = product(fold_ref[...], both)
    for r in range(rows):
        pair, side = r // 2, r % 2
        total = taps[pair, 24 + 24 * side : 48 + 24 * side]
        if side == 0 and pair > 0:
            total = total + taps[pair - 1, 72:96]
        if side == 1 and pair + 1 < half:
            total = total + taps[pair + 1, 0:24]
        both = columns_joined(total)
        for o in range(outs):
            net[o, pl.ds(jnp.where(even, r, rows - 1 - r), 1), :] = both[o : o + 1]
    push = step_factors(index_ref[0])[2]
    for t in range(width // 128):
        at = pl.ds(t * 128, 128)
        for o in range(outs):
            out_ref[o, :, at] = base_ref[o, :, at] + push * net[o, :, at]


def taps_call(first, last, top, bottom, stats, fold, base, index):
    outs, rows, width = base.shape
    chans = top.shape[1]
    return pl.pallas_call(
        taps_kernel,
        out_shape=jax.ShapeDtypeStruct(base.shape, F32),
        in_specs=[VM] * 10 + [SM],
        out_specs=VM,
        scratch_shapes=[pltpu.VMEM((width, chans), BF16)] * (rows - 2)
        + [pltpu.VMEM((rows // 2, 96, width), F32), pltpu.VMEM(base.shape, F32)],
        compiler_params=limit(24),
        cost_estimate=pl.CostEstimate(
            flops=3072 * width * chans * rows, bytes_accessed=1 << 22, transcendentals=1 << 22
        ),
        name="taps",
    )(first, last, top, bottom, *stats, fold, base, index)


def step_kernel(part_ref, core_ref, far_ref, index_ref, next_ref, blocks_ref, kept_ref):
    outs, rows, width = part_ref.shape
    even = (lax.axis_index("tile") & 1) == 0
    push = step_factors(index_ref[0])[2]
    quarter = width // 512
    line = lax.broadcasted_iota(jnp.int32, (rows, 128), 0)
    at_far = line == jnp.where(even, 0, rows - 1)
    at_core = line == jnp.where(even, rows - 1, 0)
    slot = lax.broadcasted_iota(jnp.int32, (rows, 128), 1) // 32
    for t in range(quarter):
        for o in range(outs):
            values = []
            for k in range(4):
                at = pl.ds((quarter * k + t) * 128, 128)
                extra = jnp.where(at_far, far_ref[o : o + 1, at], 0.0)
                extra = jnp.where(at_core, core_ref[o : o + 1, at], extra)
                values.append(part_ref[o, :, at] + push * extra)
                next_ref[o, :, at] = values[-1]
            for j, mixed in enumerate(turn_quarters(values, slot)):
                blocks_ref[4 * t + j, o] = mixed
                kept_ref[4 * t + j, o] = mixed


def step_call(part, core, far, index):
    outs, rows, width = part.shape
    return pl.pallas_call(
        step_kernel,
        out_shape=(
            jax.ShapeDtypeStruct(part.shape, F32),
            jax.ShapeDtypeStruct((width // 128, outs, rows, 128), F32),
            pltpu.VMEM((width // 128, outs, rows, 128), F32),
        ),
        in_specs=[VM] * 3 + [SM],
        out_specs=(VM, VM, VM),
        compiler_params=limit(8),
        name="step",
    )(part, core, far, index)


def sums_kernel(got_ref, reg_ref, out_ref):
    count = got_ref.shape[0]
    shape = got_ref.shape[2:]
    own = lax.broadcasted_iota(jnp.int32, shape, 1) // 32 == lax.axis_index("member") // count
    for o in range(got_ref.shape[1]):
        first = got_ref[0, o]
        second = first * first
        for m in range(1, count):
            value = got_ref[m, o]
            first = first + value
            second = second + value * value
        out_ref[0, o] = first
        out_ref[1, o] = second
        out_ref[2, o] = jnp.where(own, reg_ref[o], 0.0)


def sums_call(got, reg):
    return pl.pallas_call(
        sums_kernel,
        out_shape=jax.ShapeDtypeStruct((3,) + got.shape[1:], F32),
        in_specs=[VM, VM],
        out_specs=VM,
        compiler_params=limit(8),
        name="sums",
    )(got, reg)


def spread_kernel(members, one_ref, two_ref, target_ref, out_ref):
    copies, _, outs = out_ref.shape[:3]
    for o in range(outs):
        mean = (one_ref[0, o] + two_ref[0, o]) / members
        var = (one_ref[1, o] + two_ref[1, o]) / members - mean * mean
        scale = jnp.sqrt(1.0 + target_ref[o] / (var + 1.0))
        offset = one_ref[2, o] + two_ref[2, o] + mean - mean * scale
        for k in range(copies):
            out_ref[k, 0, o] = scale
            out_ref[k, 1, o] = offset


def spread_call(one, two, target, copies, members):
    return pl.pallas_call(
        functools.partial(spread_kernel, members),
        out_shape=jax.ShapeDtypeStruct((copies, 2) + one.shape[1:], F32),
        in_specs=[VM, VM, SM],
        out_specs=VM,
        compiler_params=limit(8),
        name="spread",
    )(one, two, target)


def field_kernel(blocks_ref, got_ref, out_ref):
    outs, rows, width = out_ref.shape
    quarter = width // 512
    slot = lax.broadcasted_iota(jnp.int32, (rows, 128), 1) // 32
    for t in range(quarter):
        for o in range(outs):
            values = [
                blocks_ref[4 * t + j, o] * got_ref[4 * t + j, 0, o] + got_ref[4 * t + j, 1, o] for j in range(4)
            ]
            for k, mixed in enumerate(turn_quarters(values, slot)):
                out_ref[o, :, pl.ds((quarter * k + t) * 128, 128)] = mixed


def field_call(blocks, got, shape):
    return pl.pallas_call(
        field_kernel,
        out_shape=jax.ShapeDtypeStruct(shape, F32),
        in_specs=[VM, VM],
        out_specs=VM,
        compiler_params=limit(8),
        name="field",
    )(blocks, got)


def swap(value, bits):
    return lax.ppermute(value, "tile", [(i, i ^ bits) for i in range(TILES)])


def far_swap(value):
    return lax.ppermute(value, "tile", [(1, 2), (2, 1)])


def spread_stats(stats):
    return [stats] + [swap(stats, bits) for bits in (1, 2, 3)]


def shards(
    features, residual_state, noise, regression_mean, step_index, conv_first, conv_second, head_weight, spread_target
):
    member = pltpu.with_memory_space_constraint(features[0], pltpu.HBM)
    xt, core, far, stats = features_call(member, 512)
    stats = spread_stats(stats)
    core, far = swap(core, 1), far_swap(far)
    wt, fold = weights_call(conv_first, conv_second, head_weight)
    last, sums, acts = inner_call(xt, core, stats, wt, 1024)
    first, stats = outer_call(acts, far, stats, sums, wt, 1024)
    stats = spread_stats(stats)
    base = base_call(xt, head_weight, residual_state[0], noise[0], step_index)
    core, far, top, bottom = rim_call(first, last, stats, fold)
    core, far = swap(core, 1), far_swap(far)
    part = taps_call(first, last, top, bottom, stats, fold, base, step_index)
    advanced, blocks, kept = step_call(part, core, far, step_index)
    members = lax.axis_size("member")
    size = blocks.shape[0]
    runs = [list(range(i, i + size)) for i in range(0, members, size)]
    got = lax.all_to_all(blocks, "member", 0, 0, tiled=True, axis_index_groups=runs)
    reg = jnp.tile(regression_mean, (1, 1, 4))
    sums = sums_call(got, reg)
    sums = sums + lax.ppermute(sums, "member", [(i, i ^ size) for i in range(members)])
    other = lax.ppermute(sums, "member", [(i, i ^ (3 * size)) for i in range(members)])
    sent = spread_call(sums, other, spread_target, size, members)
    got = lax.all_to_all(sent, "member", 0, 0, tiled=True, axis_index_groups=runs)
    field = field_call(kept, got, advanced.shape)
    return (field[None], advanced[None])


def solution(mesh):
    cells = P("member", None, "tile", None)
    return jax.shard_map(
        shards,
        mesh=mesh,
        in_specs=(cells, cells, cells, P(None, "tile", "member"), P(), P(), P(), P(), P()),
        out_specs=(cells, cells),
        check_vma=False,
    )
```

```python
import functools

import jax
import jax.numpy as jnp
from jax import lax
from jax.experimental import pallas as pl
from jax.experimental.pallas import tpu as pltpu
from jax.sharding import PartitionSpec as P

GROUP = 4
TILES = 4
F32, BF16 = jnp.float32, jnp.bfloat16
VM = pl.BlockSpec(memory_space=pltpu.VMEM)
SM = pl.BlockSpec(memory_space=pltpu.SMEM)


def limit(mib):
    return pltpu.CompilerParams(vmem_limit_bytes=mib * 1024 * 1024)


def group_total(row):
    lane = lax.broadcasted_iota(jnp.int32, row.shape, 1)
    size = row.shape[1]
    for step in (1, 2):
        up = pltpu.roll(row, step, 1)
        down = pltpu.roll(row, size - step, 1)
        row = row + jnp.where((lane & step) == 0, down, up)
    return row


def merged(parts, count):
    means = [p[0:1, :] for p in parts]
    devs = [p[1:2, :] for p in parts]
    members = len(parts) * GROUP
    mean = group_total(functools.reduce(jnp.add, means)) / members
    spread = functools.reduce(jnp.add, [(m - mean) * (m - mean) for m in means])
    total = group_total(functools.reduce(jnp.add, devs) + count * spread)
    return mean, lax.rsqrt(total / (members * count) + 1e-05)


def silu(values):
    half = 0.5 * values
    return half + half * jnp.tanh(half)


def row_sum(values):
    return values.reshape(-1, 8, values.shape[1]).sum(0)


def write_stats(st_ref, pivot, first, second, count):
    one = jnp.sum(first, axis=0, keepdims=True)
    two = jnp.sum(second, axis=0, keepdims=True)
    mean = pivot + one / count
    dev = two - one * one / count
    pad = jnp.zeros((6, mean.shape[1]), F32)
    st_ref[...] = jnp.concatenate([mean, dev, pad], axis=0)


def features_kernel(x_ref, xt_ref, core_ref, far_ref, st_ref, held, scr, sems):
    rows, full, chans = xt_ref.shape
    pieces, _, _, width = held.shape
    even = (lax.axis_index("tile") & 1) == 0

    def piece(i):
        at = pl.ds(pl.multiple_of(i * width, width), width)
        return pltpu.make_async_copy(x_ref.at[:, :, at], held.at[i], sems.at[i])

    for i in range(pieces):
        piece(i).start()

    def work(i, carry):
        pivot, one, two = carry
        piece(i).wait()
        for part in range(width // 128):
            at = pl.ds(pl.multiple_of(i * width + 128 * part, 128), 128)
            scr[part] = held[i, :, :, pl.ds(128 * part, 128)].astype(F32).reshape(chans * rows, 128)
            for r in range(rows):
                turned = scr[part, pl.ds(r, chans, stride=rows), :].T
                if part == 0 and r == 0:
                    pivot = jnp.where(i == 0, jnp.mean(turned, axis=0, keepdims=True), pivot)
                off = turned - pivot
                one = one + row_sum(off)
                two = two + row_sum(off * off)
                turned = turned.astype(BF16)
                xt_ref[jnp.where(even, r, rows - 1 - r), at] = turned
                if r == 0:
                    top = turned
            core_ref[at] = jnp.where(even, turned, top)
            far_ref[at] = jnp.where(even, top, turned)
        return pivot, one, two

    zero = jnp.zeros((8, chans), F32)
    pivot, one, two = lax.fori_loop(0, pieces, work, (zero[0:1], zero, zero))
    write_stats(st_ref, pivot, one, two, rows * full)


def features_call(x, block):
    chans, rows, width = x.shape
    edge = jax.ShapeDtypeStruct((width, chans), BF16)
    return pl.pallas_call(
        features_kernel,
        out_shape=(
            jax.ShapeDtypeStruct((rows, width, chans), BF16),
            edge,
            edge,
            jax.ShapeDtypeStruct((8, chans), F32),
        ),
        in_specs=[pl.BlockSpec(memory_space=pl.ANY)],
        out_specs=(VM,) * 4,
        scratch_shapes=[
            pltpu.VMEM((width // block, chans, rows, block), BF16),
            pltpu.VMEM((block // 128, chans * rows, 128), F32),
            pltpu.SemaphoreType.DMA((width // block,)),
        ],
        compiler_params=limit(16),
        name="features",
    )(x)


def step_factors(index):
    lane = lax.broadcasted_iota(jnp.int32, (8, 128), 1)
    steps = lane.astype(F32)
    upper = 800.0 ** (1.0 / 7.0)
    lower = 0.002 ** (1.0 / 7.0)
    root = upper + steps / 17.0 * (lower - upper)
    square = root * root
    sigmas = square * square * square * root
    sigma = jnp.sum(jnp.where(lane == index, sigmas, 0.0), axis=1, keepdims=True)
    follow = jnp.sum(jnp.where(lane == index + 1, sigmas, 0.0), axis=1, keepdims=True)
    sigma, follow = jnp.broadcast_to(sigma, lane.shape), jnp.broadcast_to(follow, lane.shape)
    hat = 1.25 * sigma
    spread = hat * hat + 0.25
    skip = 0.25 / spread
    gain = 0.5 * hat / jnp.sqrt(spread)
    rate = (follow - hat) / hat
    keep = 1.0 + rate - rate * skip
    return keep, keep * jnp.sqrt(hat * hat - sigma * sigma), -rate * gain


def place(even, tap):
    return jnp.where(even, tap, 3 * (2 - tap // 3) + tap % 3)


def weights_kernel(first_ref, second_ref, head_ref, wt_ref, fold_ref):
    chans = first_ref.shape[1]
    even = (lax.axis_index("tile") & 1) == 0
    wt_ref[...] = jnp.zeros(wt_ref.shape, BF16)
    for tap in range(9):
        turned = first_ref[place(even, tap)].astype(F32).T.astype(BF16)
        for q in range(2):
            row, col = tap // 3 + q, tap % 3
            wt_ref[pl.ds((3 * row + col) * chans, chans), pl.ds(q * chans, chans)] = turned
    head = jnp.concatenate([head_ref[...].astype(F32)] * 2, axis=0).astype(BF16)
    low = lax.broadcasted_iota(jnp.int32, (8, chans), 0) >= 4
    lines = []
    for row in range(3):
        parts = []
        for col in range(3):
            tap = second_ref[place(even, 3 * row + col)]
            folded = jnp.dot(head, tap, preferred_element_type=F32)
            high = folded.astype(BF16).astype(F32)
            parts.append(jnp.where(low, folded - high, high))
        lines.append(jnp.concatenate(parts, axis=0))
    none = jnp.zeros_like(lines[0])
    left = jnp.concatenate([lines[2], lines[1], lines[0], none], axis=0)
    right = jnp.concatenate([none, lines[2], lines[1], lines[0]], axis=0)
    fold_ref[...] = jnp.concatenate([left, right], axis=1).astype(BF16)


def weights_call(first, second, head):
    chans = first.shape[1]
    return pl.pallas_call(
        weights_kernel,
        out_shape=(
            jax.ShapeDtypeStruct((12 * chans, 2 * chans), BF16),
            jax.ShapeDtypeStruct((96, 2 * chans), BF16),
        ),
        in_specs=[VM] * 3,
        out_specs=(VM, VM),
        compiler_params=limit(16),
        cost_estimate=pl.CostEstimate(flops=1 << 22, bytes_accessed=1 << 21, transcendentals=0),
        name="weights",
    )(first, second, head)


def norm_factors(refs, count):
    mean, scale = merged([ref[...] for ref in refs], count)
    return scale, -mean * scale


def fill(act, buf, value, at, size):
    buf[pl.ds(at + 8, size), :] = value
    act[1, pl.ds(at, size), :] = value.astype(BF16)


def fill_sides(act, buf, at, size):
    act[0, pl.ds(at, size), :] = buf[pl.ds(at + 7, size), :].astype(BF16)
    act[2, pl.ds(at, size), :] = buf[pl.ds(at + 9, size), :].astype(BF16)


def clear_ends(buf):
    size, chans = buf.shape
    buf[pl.ds(0, 8), :] = jnp.zeros((8, chans), F32)
    buf[pl.ds(size - 8, 8), :] = jnp.zeros((8, chans), F32)


def two_rows(acts, wt_ref, at, block):
    left = jnp.concatenate([act[s, pl.ds(at, block), :] for act in acts for s in range(3)], axis=1)
    out = jnp.dot(left, wt_ref[...], preferred_element_type=F32)
    chans = out.shape[1] // 2
    return out[:, :chans], out[:, chans:]


def join(acts, wt_ref, hid_ref, lines, block, late, fresh, carry):
    width = hid_ref.shape[1]
    pivot, one, two = carry
    for at in range(0, width, block):
        a, b = two_rows(acts, wt_ref, at, block)
        if at == 0:
            for act, buf, read in late:
                rest = width - block - 16
                fill(act, buf, read(block + 16, rest), block + 16, rest)
                fill_sides(act, buf, block, width - block)
        if not late or at > 0:
            start = 0 if late else at
            size = at + block - start
            for act, buf, read in fresh:
                fill(act, buf, read(start, size), start, size)
                if start > 0:
                    fill_sides(act, buf, start - block, block)
        hid_ref[lines[0], pl.ds(at, block), :] = a.astype(BF16)
        hid_ref[lines[1], pl.ds(at, block), :] = b.astype(BF16)
        if pivot is None:
            pivot = jnp.mean(a[0:8], axis=0, keepdims=True)
        a, b = a - pivot, b - pivot
        one = one + row_sum(a + b)
        two = two + row_sum(a * a + b * b)
    for act, buf, read in fresh:
        start = 0 if late else width - block
        fill_sides(act, buf, start, width - start)
    return pivot, one, two


def inner_kernel(block, x_ref, core_ref, s0, s1, s2, s3, wt_ref, hid_ref, sum_ref, *rest):
    rows, width, chans = x_ref.shape
    acts, bufs = rest[: rows + 1], rest[rows + 1 :]
    scale, shift = norm_factors([s0, s1, s2, s3], rows * width)
    for buf in bufs:
        clear_ends(buf)

    def line(row):
        def read(at, size):
            span = pl.ds(at, size)
            value = core_ref[span, :] if row == rows else x_ref[row, span, :]
            return silu(value.astype(F32) * scale + shift)

        return acts[row], bufs[row % len(bufs)], read

    early = [line(row) for row in range(1, 5)]
    for act, buf, read in early:
        fill(act, buf, read(0, block + 16), 0, block + 16)
        fill_sides(act, buf, 0, block)
    zero = jnp.zeros((8, chans), F32)
    carry = (None, zero, zero)
    for pair, fresh in ((0, (5, 6)), (1, (7, 8)), (2, (0,))):
        group = acts[2 * pair + 1 : 2 * pair + 5]
        lines = (2 * pair, 2 * pair + 1)
        fresh = [line(row) for row in fresh]
        carry = join(group, wt_ref, hid_ref, lines, block, early if pair == 0 else [], fresh, carry)
    pivot, one, two = carry
    sum_ref[0] = jnp.broadcast_to(pivot, one.shape)
    sum_ref[1] = one
    sum_ref[2] = two


def inner_call(xt, core, stats, wt, block):
    rows, width, chans = xt.shape
    act = jax.ShapeDtypeStruct((3, width, chans), BF16)
    hid, sums, *acts = pl.pallas_call(
        functools.partial(inner_kernel, block),
        out_shape=(
            jax.ShapeDtypeStruct((rows - 2, width, chans), BF16),
            jax.ShapeDtypeStruct((3, 8, chans), F32),
            act,
            act,
            act,
        ),
        in_specs=[VM] * 7,
        out_specs=(VM,) * 5,
        scratch_shapes=[pltpu.VMEM(act.shape, BF16)] * (rows - 2)
        + [pltpu.VMEM((width + 16, chans), F32)] * 4,
        compiler_params=limit(32),
        cost_estimate=pl.CostEstimate(
            flops=24 * rows * width * chans * chans, bytes_accessed=1 << 22, transcendentals=xt.size
        ),
        name="inner",
    )(xt, core, *stats, wt)
    return hid, sums, acts


def outer_kernel(block, far_ref, a0, a1, a2, s0, s1, s2, s3, sum_ref, wt_ref, hid_ref, st_ref, act, buf):
    width, chans = far_ref.shape
    tile = lax.axis_index("tile")
    linked = ((tile == 1) | (tile == 2)).astype(F32)
    count = TILES * 2 * width
    scale, shift = norm_factors([s0, s1, s2, s3], count)
    clear_ends(buf)

    def read(at, size):
        return silu(far_ref[pl.ds(at, size), :].astype(F32) * scale + shift) * linked

    fill(act, buf, read(0, block + 16), 0, block + 16)
    fill_sides(act, buf, 0, block)
    carry = (sum_ref[0, 0:1], sum_ref[1], sum_ref[2])
    early = [(act, buf, read)]
    pivot, one, two = join([act, a0, a1, a2], wt_ref, hid_ref, (0, 1), block, early, [], carry)
    write_stats(st_ref, pivot, one, two, count)


def outer_call(acts, far, stats, sums, wt, block):
    width, chans = far.shape
    return pl.pallas_call(
        functools.partial(outer_kernel, block),
        out_shape=(
            jax.ShapeDtypeStruct((2, width, chans), BF16),
            jax.ShapeDtypeStruct((8, chans), F32),
        ),
        in_specs=[VM] * 10,
        out_specs=(VM,) * 2,
        scratch_shapes=[pltpu.VMEM((3, width, chans), BF16), pltpu.VMEM((width + 16, chans), F32)],
        compiler_params=limit(12),
        name="outer",
    )(far, *acts, *stats, sums, wt)


def turn_quarters(values, slot):
    low, right = slot < 2, (slot & 1) == 0
    halves = []
    for a, b in ((values[0], values[2]), (values[1], values[3])):
        moved = pltpu.roll(jnp.where(low, b, a), 64, 1)
        halves.append((jnp.where(low, a, moved), jnp.where(low, moved, b)))
    out = [None] * 4
    for k in range(2):
        a, b = halves[0][k], halves[1][k]
        out[2 * k] = jnp.where(right, a, pltpu.roll(b, 32, 1))
        out[2 * k + 1] = jnp.where(right, pltpu.roll(a, 96, 1), b)
    return out


def columns_joined(total):
    width = total.shape[1]
    lane = lax.broadcasted_iota(jnp.int32, (8, width), 1)
    left = jnp.where(lane == 0, 0.0, pltpu.roll(total[0:8], 1, 1))
    right = jnp.where(lane == width - 1, 0.0, pltpu.roll(total[16:24], width - 1, 1))
    both = left + total[8:16] + right
    return both[0:4] + both[4:8]


def product(left, right):
    return lax.dot_general(left, right, (((1,), (1,)), ((), ())), preferred_element_type=F32)


def rim_kernel(first_ref, last_ref, s0, s1, s2, s3, fold_ref, core_ref, far_ref, top_ref, bottom_ref):
    width, chans = top_ref.shape
    scale, shift = norm_factors([s0, s1, s2, s3], TILES * 2 * width)
    value = silu(first_ref[0].astype(F32) * scale + shift)
    top_ref[...] = value.astype(BF16)
    value = silu(last_ref[last_ref.shape[0] - 1].astype(F32) * scale + shift)
    bottom_ref[...] = value.astype(BF16)
    none = jnp.zeros((24, chans), BF16)
    before = jnp.concatenate([fold_ref[0:24, :chans], none], axis=1)
    after = jnp.concatenate([none, fold_ref[72:96, chans:]], axis=1)
    both = jnp.concatenate([top_ref[...], bottom_ref[...]], axis=1)
    ends = product(jnp.concatenate([before, after], axis=0), both)
    far_ref[...] = columns_joined(ends[0:24])
    core_ref[...] = columns_joined(ends[24:48])


def rim_call(first, last, stats, fold):
    width, chans = first.shape[1:]
    part = jax.ShapeDtypeStruct((4, width), F32)
    act = jax.ShapeDtypeStruct((width, chans), BF16)
    return pl.pallas_call(
        rim_kernel,
        out_shape=(part, part, act, act),
        in_specs=[VM] * 7,
        out_specs=(VM,) * 4,
        compiler_params=limit(8),
        name="rim",
    )(first, last, *stats, fold)


def base_kernel(x_ref, head_ref, state_ref, noise_ref, index_ref, out_ref, net):
    rows, width, _ = x_ref.shape
    outs = state_ref.shape[0]
    even = (lax.axis_index("tile") & 1) == 0
    head = head_ref[...].astype(F32)
    head = jnp.concatenate([head, jnp.zeros_like(head)], axis=0)
    none = jnp.zeros_like(head)
    head = jnp.concatenate(
        [jnp.concatenate([head, none], axis=1), jnp.concatenate([none, head], axis=1)], axis=0
    ).astype(BF16)
    for pair in range(rows // 2):
        features = jnp.concatenate([x_ref[2 * pair], x_ref[2 * pair + 1]], axis=1)
        both = product(head, features)
        for side in range(2):
            r = 2 * pair + side
            for o in range(outs):
                line = both[8 * side + o : 8 * side + o + 1]
                net[o, pl.ds(jnp.where(even, r, rows - 1 - r), 1), :] = line
    keep, stir, push = step_factors(index_ref[0])
    for t in range(width // 128):
        at = pl.ds(t * 128, 128)
        for o in range(outs):
            direct = keep * state_ref[o, :, at] + stir * noise_ref[o, :, at]
            out_ref[o, :, at] = direct + push * net[o, :, at]


def base_call(xt, head, state, noise, index):
    return pl.pallas_call(
        base_kernel,
        out_shape=jax.ShapeDtypeStruct(state.shape, F32),
        in_specs=[VM] * 4 + [SM],
        out_specs=VM,
        scratch_shapes=[pltpu.VMEM(state.shape, F32)],
        compiler_params=limit(12),
        cost_estimate=pl.CostEstimate(flops=1 << 24, bytes_accessed=1 << 20, transcendentals=0),
        name="base",
    )(xt, head, state, noise, index)


def taps_kernel(first_ref, last_ref, top_ref, bottom_ref, s0, s1, s2, s3, fold_ref, base_ref, index_ref, out_ref, *rest):
    outs, rows, width = base_ref.shape
    half = rows // 2
    acts, taps, net = rest[: rows - 2], rest[rows - 2], rest[rows - 1]
    acts = (top_ref,) + acts + (bottom_ref,)
    even = (lax.axis_index("tile") & 1) == 0
    scale, shift = norm_factors([s0, s1, s2, s3], rows * width)
    for pair in range(half):
        for row in (2 * pair, 2 * pair + 1):
            if 0 < row < rows - 1:
                value = first_ref[row] if row < 2 else last_ref[row - 2]
                acts[row][...] = silu(value.astype(F32) * scale + shift).astype(BF16)
        both = jnp.concatenate([acts[2 * pair][...], acts[2 * pair + 1][...]], axis=1)
        taps[pair] = product(fold_ref[...], both)
    for r in range(rows):
        pair, side = r // 2, r % 2
        total = taps[pair, 24 + 24 * side : 48 + 24 * side]
        if side == 0 and pair > 0:
            total = total + taps[pair - 1, 72:96]
        if side == 1 and pair + 1 < half:
            total = total + taps[pair + 1, 0:24]
        both = columns_joined(total)
        for o in range(outs):
            net[o, pl.ds(jnp.where(even, r, rows - 1 - r), 1), :] = both[o : o + 1]
    push = step_factors(index_ref[0])[2]
    for t in range(width // 128):
        at = pl.ds(t * 128, 128)
        for o in range(outs):
            out_ref[o, :, at] = base_ref[o, :, at] + push * net[o, :, at]


def taps_call(first, last, top, bottom, stats, fold, base, index):
    outs, rows, width = base.shape
    chans = top.shape[1]
    return pl.pallas_call(
        taps_kernel,
        out_shape=jax.ShapeDtypeStruct(base.shape, F32),
        in_specs=[VM] * 10 + [SM],
        out_specs=VM,
        scratch_shapes=[pltpu.VMEM((width, chans), BF16)] * (rows - 2)
        + [pltpu.VMEM((rows // 2, 96, width), F32), pltpu.VMEM(base.shape, F32)],
        compiler_params=limit(24),
        cost_estimate=pl.CostEstimate(
            flops=3072 * width * chans * rows, bytes_accessed=1 << 22, transcendentals=1 << 22
        ),
        name="taps",
    )(first, last, top, bottom, *stats, fold, base, index)


def step_kernel(part_ref, core_ref, far_ref, index_ref, next_ref, blocks_ref, kept_ref):
    outs, rows, width = part_ref.shape
    even = (lax.axis_index("tile") & 1) == 0
    push = step_factors(index_ref[0])[2]
    quarter = width // 512
    line = lax.broadcasted_iota(jnp.int32, (rows, 128), 0)
    at_far = line == jnp.where(even, 0, rows - 1)
    at_core = line == jnp.where(even, rows - 1, 0)
    slot = lax.broadcasted_iota(jnp.int32, (rows, 128), 1) // 32
    for t in range(quarter):
        for o in range(outs):
            values = []
            for k in range(4):
                at = pl.ds((quarter * k + t) * 128, 128)
                extra = jnp.where(at_far, far_ref[o : o + 1, at], 0.0)
                extra = jnp.where(at_core, core_ref[o : o + 1, at], extra)
                values.append(part_ref[o, :, at] + push * extra)
                next_ref[o, :, at] = values[-1]
            for j, mixed in enumerate(turn_quarters(values, slot)):
                blocks_ref[4 * t + j, o] = mixed
                kept_ref[4 * t + j, o] = mixed


def step_call(part, core, far, index):
    outs, rows, width = part.shape
    return pl.pallas_call(
        step_kernel,
        out_shape=(
            jax.ShapeDtypeStruct(part.shape, F32),
            jax.ShapeDtypeStruct((width // 128, outs, rows, 128), F32),
            pltpu.VMEM((width // 128, outs, rows, 128), F32),
        ),
        in_specs=[VM] * 3 + [SM],
        out_specs=(VM, VM, VM),
        compiler_params=limit(8),
        name="step",
    )(part, core, far, index)


def sums_kernel(got_ref, reg_ref, out_ref):
    count = got_ref.shape[0]
    shape = got_ref.shape[2:]
    own = lax.broadcasted_iota(jnp.int32, shape, 1) // 32 == lax.axis_index("member") // count
    for o in range(got_ref.shape[1]):
        first = got_ref[0, o]
        second = first * first
        for m in range(1, count):
            value = got_ref[m, o]
            first = first + value
            second = second + value * value
        out_ref[0, o] = first
        out_ref[1, o] = second
        out_ref[2, o] = jnp.where(own, reg_ref[o], 0.0)


def sums_call(got, reg):
    return pl.pallas_call(
        sums_kernel,
        out_shape=jax.ShapeDtypeStruct((3,) + got.shape[1:], F32),
        in_specs=[VM, VM],
        out_specs=VM,
        compiler_params=limit(8),
        name="sums",
    )(got, reg)


STEPS = 32000.0


def coded(values):
    top = jnp.max(jnp.max(jnp.abs(values), axis=1, keepdims=True), axis=0, keepdims=True)
    power = jnp.clip(jnp.ceil(jnp.log2(jnp.maximum(top, 1e-30))), -100.0, 127.0)
    power = jnp.broadcast_to(power, (1, values.shape[1]))
    return jnp.round(values / jnp.exp2(power) * STEPS), power


def as_words(values):
    return values.astype(jnp.int32).astype(jnp.int16)


def as_floats(words):
    return words.astype(jnp.int32).astype(F32)


def spread_kernel(members, one_ref, two_ref, target_ref, out_ref):
    copies, count = out_ref.shape[:2]
    outs = count - 1
    words, powers = [], []
    for o in range(outs):
        mean = (one_ref[0, o] + two_ref[0, o]) / members
        var = (one_ref[1, o] + two_ref[1, o]) / members - mean * mean
        scale = jnp.sqrt(1.0 + target_ref[o] / (var + 1.0))
        offset = one_ref[2, o] + two_ref[2, o] + mean - mean * scale
        high, high_power = coded(scale - 1.0)
        low, low_power = coded(offset)
        words.append(as_words(jnp.concatenate([high, low], axis=0)))
        powers += [high_power, low_power]
    rest = jnp.zeros((16 - len(powers), powers[0].shape[1]), F32)
    words.append(as_words(jnp.concatenate(powers + [rest], axis=0)))
    for k in range(copies):
        for o in range(count):
            out_ref[k, o] = words[o]


def spread_call(one, two, target, copies, members):
    _, outs, rows, lanes = one.shape
    return pl.pallas_call(
        functools.partial(spread_kernel, members),
        out_shape=jax.ShapeDtypeStruct((copies, outs + 1, 2 * rows, lanes), jnp.int16),
        in_specs=[VM, VM, SM],
        out_specs=VM,
        compiler_params=limit(8),
        name="spread",
    )(one, two, target)


def field_kernel(blocks_ref, got_ref, out_ref):
    outs, rows, width = out_ref.shape
    quarter = width // 512
    slot = lax.broadcasted_iota(jnp.int32, (rows, 128), 1) // 32
    for t in range(quarter):
        units = [jnp.exp2(as_floats(got_ref[4 * t + j, outs])) / STEPS for j in range(4)]
        for o in range(outs):
            values = []
            for j in range(4):
                words = as_floats(got_ref[4 * t + j, o])
                scale = 1.0 + words[:rows] * units[j][2 * o : 2 * o + 1]
                offset = words[rows:] * units[j][2 * o + 1 : 2 * o + 2]
                values.append(blocks_ref[4 * t + j, o] * scale + offset)
            for k, mixed in enumerate(turn_quarters(values, slot)):
                out_ref[o, :, pl.ds((quarter * k + t) * 128, 128)] = mixed


def field_call(blocks, got, shape):
    return pl.pallas_call(
        field_kernel,
        out_shape=jax.ShapeDtypeStruct(shape, F32),
        in_specs=[VM, VM],
        out_specs=VM,
        compiler_params=limit(8),
        name="field",
    )(blocks, got)


def swap(value, bits):
    return lax.ppermute(value, "tile", [(i, i ^ bits) for i in range(TILES)])


def far_swap(value):
    return lax.ppermute(value, "tile", [(1, 2), (2, 1)])


def spread_stats(stats):
    return [stats] + [swap(stats, bits) for bits in (1, 2, 3)]


def shards(
    features, residual_state, noise, regression_mean, step_index, conv_first, conv_second, head_weight, spread_target
):
    member = pltpu.with_memory_space_constraint(features[0], pltpu.HBM)
    xt, core, far, stats = features_call(member, 512)
    stats = spread_stats(stats)
    core, far = swap(core, 1), far_swap(far)
    wt, fold = weights_call(conv_first, conv_second, head_weight)
    last, sums, acts = inner_call(xt, core, stats, wt, 1024)
    first, stats = outer_call(acts, far, stats, sums, wt, 1024)
    stats = spread_stats(stats)
    base = base_call(xt, head_weight, residual_state[0], noise[0], step_index)
    core, far, top, bottom = rim_call(first, last, stats, fold)
    core, far = swap(core, 1), far_swap(far)
    part = taps_call(first, last, top, bottom, stats, fold, base, step_index)
    advanced, blocks, kept = step_call(part, core, far, step_index)
    members = lax.axis_size("member")
    size = blocks.shape[0]
    runs = [list(range(i, i + size)) for i in range(0, members, size)]
    got = lax.all_to_all(blocks, "member", 0, 0, tiled=True, axis_index_groups=runs)
    reg = jnp.tile(regression_mean, (1, 1, 4))
    sums = sums_call(got, reg)
    sums = sums + lax.ppermute(sums, "member", [(i, i ^ size) for i in range(members)])
    other = lax.ppermute(sums, "member", [(i, i ^ (3 * size)) for i in range(members)])
    sent = spread_call(sums, other, spread_target, size, members)
    got = lax.all_to_all(sent, "member", 0, 0, tiled=True, axis_index_groups=runs)
    field = field_call(kept, got, advanced.shape)
    return (field[None], advanced[None])


def solution(mesh):
    cells = P("member", None, "tile", None)
    return jax.shard_map(
        shards,
        mesh=mesh,
        in_specs=(cells, cells, cells, P(None, "tile", "member"), P(), P(), P(), P(), P()),
        out_specs=(cells, cells),
        check_vma=False,
    )
```

```python
import functools

import jax
import jax.numpy as jnp
from jax import lax
from jax.experimental import pallas as pl
from jax.experimental.pallas import tpu as pltpu
from jax.sharding import PartitionSpec as P

GROUP = 4
TILES = 4
F32, BF16 = jnp.float32, jnp.bfloat16
VM = pl.BlockSpec(memory_space=pltpu.VMEM)
SM = pl.BlockSpec(memory_space=pltpu.SMEM)


def limit(mib):
    return pltpu.CompilerParams(vmem_limit_bytes=mib * 1024 * 1024)


def group_total(row):
    lane = lax.broadcasted_iota(jnp.int32, row.shape, 1)
    size = row.shape[1]
    for step in (1, 2):
        up = pltpu.roll(row, step, 1)
        down = pltpu.roll(row, size - step, 1)
        row = row + jnp.where((lane & step) == 0, down, up)
    return row


def merged(parts, count):
    means = [p[0:1, :] for p in parts]
    devs = [p[1:2, :] for p in parts]
    members = len(parts) * GROUP
    mean = group_total(functools.reduce(jnp.add, means)) / members
    spread = functools.reduce(jnp.add, [(m - mean) * (m - mean) for m in means])
    total = group_total(functools.reduce(jnp.add, devs) + count * spread)
    return mean, lax.rsqrt(total / (members * count) + 1e-05)


def silu(values):
    half = 0.5 * values
    return half + half * jnp.tanh(half)


def row_sum(values):
    return values.reshape(-1, 8, values.shape[1]).sum(0)


def write_stats(st_ref, pivot, first, second, count):
    one = jnp.sum(first, axis=0, keepdims=True)
    two = jnp.sum(second, axis=0, keepdims=True)
    mean = pivot + one / count
    dev = two - one * one / count
    pad = jnp.zeros((6, mean.shape[1]), F32)
    st_ref[...] = jnp.concatenate([mean, dev, pad], axis=0)


def features_kernel(x_ref, xt_ref, core_ref, far_ref, st_ref, held, scr, sems):
    rows, full, chans = xt_ref.shape
    pieces, _, _, width = held.shape
    even = (lax.axis_index("tile") & 1) == 0

    def piece(i):
        at = pl.ds(pl.multiple_of(i * width, width), width)
        return pltpu.make_async_copy(x_ref.at[:, :, at], held.at[i], sems.at[i])

    for i in range(pieces):
        piece(i).start()

    def work(i, carry):
        pivot, one, two = carry
        piece(i).wait()
        for part in range(width // 128):
            at = pl.ds(pl.multiple_of(i * width + 128 * part, 128), 128)
            scr[part] = held[i, :, :, pl.ds(128 * part, 128)].astype(F32).reshape(chans * rows, 128)
            for r in range(rows):
                turned = scr[part, pl.ds(r, chans, stride=rows), :].T
                if part == 0 and r == 0:
                    pivot = jnp.where(i == 0, jnp.mean(turned, axis=0, keepdims=True), pivot)
                off = turned - pivot
                one = one + row_sum(off)
                two = two + row_sum(off * off)
                turned = turned.astype(BF16)
                xt_ref[jnp.where(even, r, rows - 1 - r), at] = turned
                if r == 0:
                    top = turned
            core_ref[at] = jnp.where(even, turned, top)
            far_ref[at] = jnp.where(even, top, turned)
        return pivot, one, two

    zero = jnp.zeros((8, chans), F32)
    pivot, one, two = lax.fori_loop(0, pieces, work, (zero[0:1], zero, zero))
    write_stats(st_ref, pivot, one, two, rows * full)


def features_call(x, block):
    chans, rows, width = x.shape
    edge = jax.ShapeDtypeStruct((width, chans), BF16)
    return pl.pallas_call(
        features_kernel,
        out_shape=(
            jax.ShapeDtypeStruct((rows, width, chans), BF16),
            edge,
            edge,
            jax.ShapeDtypeStruct((8, chans), F32),
        ),
        in_specs=[pl.BlockSpec(memory_space=pl.ANY)],
        out_specs=(VM,) * 4,
        scratch_shapes=[
            pltpu.VMEM((width // block, chans, rows, block), BF16),
            pltpu.VMEM((block // 128, chans * rows, 128), F32),
            pltpu.SemaphoreType.DMA((width // block,)),
        ],
        compiler_params=limit(16),
        name="features",
    )(x)


def step_factors(index):
    lane = lax.broadcasted_iota(jnp.int32, (8, 128), 1)
    steps = lane.astype(F32)
    upper = 800.0 ** (1.0 / 7.0)
    lower = 0.002 ** (1.0 / 7.0)
    root = upper + steps / 17.0 * (lower - upper)
    square = root * root
    sigmas = square * square * square * root
    sigma = jnp.sum(jnp.where(lane == index, sigmas, 0.0), axis=1, keepdims=True)
    follow = jnp.sum(jnp.where(lane == index + 1, sigmas, 0.0), axis=1, keepdims=True)
    sigma, follow = jnp.broadcast_to(sigma, lane.shape), jnp.broadcast_to(follow, lane.shape)
    hat = 1.25 * sigma
    spread = hat * hat + 0.25
    skip = 0.25 / spread
    gain = 0.5 * hat / jnp.sqrt(spread)
    rate = (follow - hat) / hat
    keep = 1.0 + rate - rate * skip
    return keep, keep * jnp.sqrt(hat * hat - sigma * sigma), -rate * gain


def place(even, tap):
    return jnp.where(even, tap, 3 * (2 - tap // 3) + tap % 3)


def weights_kernel(first_ref, second_ref, head_ref, wt_ref, fold_ref, ends_ref):
    chans = first_ref.shape[1]
    even = (lax.axis_index("tile") & 1) == 0
    wt_ref[...] = jnp.zeros(wt_ref.shape, BF16)
    for tap in range(9):
        turned = first_ref[place(even, tap)].astype(F32).T.astype(BF16)
        for q in range(2):
            row, col = tap // 3 + q, tap % 3
            wt_ref[pl.ds((3 * row + col) * chans, chans), pl.ds(q * chans, chans)] = turned
    head = jnp.concatenate([head_ref[...].astype(F32)] * 2, axis=0).astype(BF16)
    low = lax.broadcasted_iota(jnp.int32, (8, chans), 0) >= 4
    lines = []
    for row in range(3):
        parts = []
        for col in range(3):
            tap = second_ref[place(even, 3 * row + col)]
            folded = jnp.dot(head, tap, preferred_element_type=F32)
            high = folded.astype(BF16).astype(F32)
            parts.append(jnp.where(low, folded - high, high))
        lines.append(jnp.concatenate(parts, axis=0))
    none = jnp.zeros_like(lines[0])
    left = jnp.concatenate([lines[2], lines[1], lines[0], none], axis=0)
    right = jnp.concatenate([none, lines[2], lines[1], lines[0]], axis=0)
    fold_ref[...] = jnp.concatenate([left, right], axis=1).astype(BF16)
    left = jnp.concatenate([lines[2], none], axis=0)
    right = jnp.concatenate([none, lines[0]], axis=0)
    ends_ref[...] = jnp.concatenate([left, right], axis=1).astype(BF16)


def weights_call(first, second, head):
    chans = first.shape[1]
    return pl.pallas_call(
        weights_kernel,
        out_shape=(
            jax.ShapeDtypeStruct((12 * chans, 2 * chans), BF16),
            jax.ShapeDtypeStruct((96, 2 * chans), BF16),
            jax.ShapeDtypeStruct((48, 2 * chans), BF16),
        ),
        in_specs=[VM] * 3,
        out_specs=(VM, VM, VM),
        compiler_params=limit(16),
        cost_estimate=pl.CostEstimate(flops=1 << 22, bytes_accessed=1 << 21, transcendentals=0),
        name="weights",
    )(first, second, head)


def norm_factors(refs, count):
    mean, scale = merged([ref[...] for ref in refs], count)
    return scale, -mean * scale


def fill(act, buf, value, at, size):
    buf[pl.ds(at + 8, size), :] = value
    act[1, pl.ds(at, size), :] = value.astype(BF16)


def fill_sides(act, buf, at, size):
    act[0, pl.ds(at, size), :] = buf[pl.ds(at + 7, size), :].astype(BF16)
    act[2, pl.ds(at, size), :] = buf[pl.ds(at + 9, size), :].astype(BF16)


def clear_ends(buf):
    size, chans = buf.shape
    buf[pl.ds(0, 8), :] = jnp.zeros((8, chans), F32)
    buf[pl.ds(size - 8, 8), :] = jnp.zeros((8, chans), F32)


def two_rows(acts, wt_ref, at, block):
    left = jnp.concatenate([act[s, pl.ds(at, block), :] for act in acts for s in range(3)], axis=1)
    out = jnp.dot(left, wt_ref[...], preferred_element_type=F32)
    chans = out.shape[1] // 2
    return out[:, :chans], out[:, chans:]


def join(acts, wt_ref, hid_ref, lines, block, late, fresh, carry):
    width = hid_ref.shape[1]
    pivot, one, two = carry
    for at in range(0, width, block):
        a, b = two_rows(acts, wt_ref, at, block)
        if at == 0:
            for act, buf, read in late:
                rest = width - block - 16
                fill(act, buf, read(block + 16, rest), block + 16, rest)
                fill_sides(act, buf, block, width - block)
        if not late or at > 0:
            start = 0 if late else at
            size = at + block - start
            for act, buf, read in fresh:
                fill(act, buf, read(start, size), start, size)
                if start > 0:
                    fill_sides(act, buf, start - block, block)
        hid_ref[lines[0], pl.ds(at, block), :] = a.astype(BF16)
        hid_ref[lines[1], pl.ds(at, block), :] = b.astype(BF16)
        if pivot is None:
            pivot = jnp.mean(a[0:8], axis=0, keepdims=True)
        a, b = a - pivot, b - pivot
        one = one + row_sum(a + b)
        two = two + row_sum(a * a + b * b)
    for act, buf, read in fresh:
        start = 0 if late else width - block
        fill_sides(act, buf, start, width - start)
    return pivot, one, two


def inner_kernel(block, x_ref, core_ref, s0, s1, s2, s3, wt_ref, hid_ref, sum_ref, *rest):
    rows, width, chans = x_ref.shape
    acts, bufs = rest[: rows + 1], rest[rows + 1 :]
    scale, shift = norm_factors([s0, s1, s2, s3], rows * width)
    for buf in bufs:
        clear_ends(buf)

    def line(row):
        def read(at, size):
            span = pl.ds(at, size)
            value = core_ref[span, :] if row == rows else x_ref[row, span, :]
            return silu(value.astype(F32) * scale + shift)

        return acts[row], bufs[row % len(bufs)], read

    early = [line(row) for row in range(1, 5)]
    for act, buf, read in early:
        fill(act, buf, read(0, block + 16), 0, block + 16)
        fill_sides(act, buf, 0, block)
    zero = jnp.zeros((8, chans), F32)
    carry = (None, zero, zero)
    for pair, fresh in ((0, (5, 6)), (1, (7, 8)), (2, (0,))):
        group = acts[2 * pair + 1 : 2 * pair + 5]
        lines = (2 * pair, 2 * pair + 1)
        fresh = [line(row) for row in fresh]
        carry = join(group, wt_ref, hid_ref, lines, block, early if pair == 0 else [], fresh, carry)
    pivot, one, two = carry
    sum_ref[0] = jnp.broadcast_to(pivot, one.shape)
    sum_ref[1] = one
    sum_ref[2] = two


def inner_call(xt, core, stats, wt, block):
    rows, width, chans = xt.shape
    act = jax.ShapeDtypeStruct((3, width, chans), BF16)
    hid, sums, *acts = pl.pallas_call(
        functools.partial(inner_kernel, block),
        out_shape=(
            jax.ShapeDtypeStruct((rows - 2, width, chans), BF16),
            jax.ShapeDtypeStruct((3, 8, chans), F32),
            act,
            act,
            act,
        ),
        in_specs=[VM] * 7,
        out_specs=(VM,) * 5,
        scratch_shapes=[pltpu.VMEM(act.shape, BF16)] * (rows - 2)
        + [pltpu.VMEM((width + 16, chans), F32)] * 4,
        compiler_params=limit(32),
        cost_estimate=pl.CostEstimate(
            flops=24 * rows * width * chans * chans, bytes_accessed=1 << 22, transcendentals=xt.size
        ),
        name="inner",
    )(xt, core, *stats, wt)
    return hid, sums, acts


def outer_kernel(block, far_ref, a0, a1, a2, s0, s1, s2, s3, sum_ref, wt_ref, hid_ref, st_ref, act, buf):
    width, chans = far_ref.shape
    tile = lax.axis_index("tile")
    linked = ((tile == 1) | (tile == 2)).astype(F32)
    count = TILES * 2 * width
    scale, shift = norm_factors([s0, s1, s2, s3], count)
    clear_ends(buf)

    def read(at, size):
        return silu(far_ref[pl.ds(at, size), :].astype(F32) * scale + shift) * linked

    fill(act, buf, read(0, block + 16), 0, block + 16)
    fill_sides(act, buf, 0, block)
    carry = (sum_ref[0, 0:1], sum_ref[1], sum_ref[2])
    early = [(act, buf, read)]
    pivot, one, two = join([act, a0, a1, a2], wt_ref, hid_ref, (0, 1), block, early, [], carry)
    write_stats(st_ref, pivot, one, two, count)


def outer_call(acts, far, stats, sums, wt, block):
    width, chans = far.shape
    return pl.pallas_call(
        functools.partial(outer_kernel, block),
        out_shape=(
            jax.ShapeDtypeStruct((2, width, chans), BF16),
            jax.ShapeDtypeStruct((8, chans), F32),
        ),
        in_specs=[VM] * 10,
        out_specs=(VM,) * 2,
        scratch_shapes=[pltpu.VMEM((3, width, chans), BF16), pltpu.VMEM((width + 16, chans), F32)],
        compiler_params=limit(12),
        name="outer",
    )(far, *acts, *stats, sums, wt)


def turn_quarters(values, slot):
    low, right = slot < 2, (slot & 1) == 0
    halves = []
    for a, b in ((values[0], values[2]), (values[1], values[3])):
        moved = pltpu.roll(jnp.where(low, b, a), 64, 1)
        halves.append((jnp.where(low, a, moved), jnp.where(low, moved, b)))
    out = [None] * 4
    for k in range(2):
        a, b = halves[0][k], halves[1][k]
        out[2 * k] = jnp.where(right, a, pltpu.roll(b, 32, 1))
        out[2 * k + 1] = jnp.where(right, pltpu.roll(a, 96, 1), b)
    return out


def columns_joined(total):
    width = total.shape[1]
    lane = lax.broadcasted_iota(jnp.int32, (8, width), 1)
    left = jnp.where(lane == 0, 0.0, pltpu.roll(total[0:8], 1, 1))
    right = jnp.where(lane == width - 1, 0.0, pltpu.roll(total[16:24], width - 1, 1))
    both = left + total[8:16] + right
    return both[0:4] + both[4:8]


def product(left, right):
    return lax.dot_general(left, right, (((1,), (1,)), ((), ())), preferred_element_type=F32)


def rim_kernel(first_ref, last_ref, s0, s1, s2, s3, ends_ref, core_ref, far_ref, top_ref, bottom_ref):
    width, chans = top_ref.shape
    scale, shift = norm_factors([s0, s1, s2, s3], TILES * 2 * width)
    value = silu(first_ref[0].astype(F32) * scale + shift)
    top_ref[...] = value.astype(BF16)
    value = silu(last_ref[last_ref.shape[0] - 1].astype(F32) * scale + shift)
    bottom_ref[...] = value.astype(BF16)
    both = jnp.concatenate([top_ref[...], bottom_ref[...]], axis=1)
    ends = product(ends_ref[...], both)
    far_ref[...] = columns_joined(ends[0:24])
    core_ref[...] = columns_joined(ends[24:48])


def rim_call(first, last, stats, ends):
    width, chans = first.shape[1:]
    part = jax.ShapeDtypeStruct((4, width), F32)
    act = jax.ShapeDtypeStruct((width, chans), BF16)
    return pl.pallas_call(
        rim_kernel,
        out_shape=(part, part, act, act),
        in_specs=[VM] * 7,
        out_specs=(VM,) * 4,
        compiler_params=limit(8),
        name="rim",
    )(first, last, *stats, ends)


def base_kernel(x_ref, head_ref, state_ref, noise_ref, index_ref, out_ref, net):
    rows, width, _ = x_ref.shape
    outs = state_ref.shape[0]
    even = (lax.axis_index("tile") & 1) == 0
    head = head_ref[...].astype(F32)
    head = jnp.concatenate([head, jnp.zeros_like(head)], axis=0)
    none = jnp.zeros_like(head)
    head = jnp.concatenate(
        [jnp.concatenate([head, none], axis=1), jnp.concatenate([none, head], axis=1)], axis=0
    ).astype(BF16)
    for pair in range(rows // 2):
        features = jnp.concatenate([x_ref[2 * pair], x_ref[2 * pair + 1]], axis=1)
        both = product(head, features)
        for side in range(2):
            r = 2 * pair + side
            for o in range(outs):
                line = both[8 * side + o : 8 * side + o + 1]
                net[o, pl.ds(jnp.where(even, r, rows - 1 - r), 1), :] = line
    keep, stir, push = step_factors(index_ref[0])
    for t in range(width // 128):
        at = pl.ds(t * 128, 128)
        for o in range(outs):
            direct = keep * state_ref[o, :, at] + stir * noise_ref[o, :, at]
            out_ref[o, :, at] = direct + push * net[o, :, at]


def base_call(xt, head, state, noise, index):
    return pl.pallas_call(
        base_kernel,
        out_shape=jax.ShapeDtypeStruct(state.shape, F32),
        in_specs=[VM] * 4 + [SM],
        out_specs=VM,
        scratch_shapes=[pltpu.VMEM(state.shape, F32)],
        compiler_params=limit(12),
        cost_estimate=pl.CostEstimate(flops=1 << 24, bytes_accessed=1 << 20, transcendentals=0),
        name="base",
    )(xt, head, state, noise, index)


def taps_kernel(first_ref, last_ref, top_ref, bottom_ref, s0, s1, s2, s3, fold_ref, base_ref, index_ref, out_ref, *rest):
    outs, rows, width = base_ref.shape
    half = rows // 2
    acts, taps, net = rest[: rows - 2], rest[rows - 2], rest[rows - 1]
    acts = (top_ref,) + acts + (bottom_ref,)
    even = (lax.axis_index("tile") & 1) == 0
    scale, shift = norm_factors([s0, s1, s2, s3], rows * width)
    for pair in range(half):
        for row in (2 * pair, 2 * pair + 1):
            if 0 < row < rows - 1:
                value = first_ref[row] if row < 2 else last_ref[row - 2]
                acts[row][...] = silu(value.astype(F32) * scale + shift).astype(BF16)
        both = jnp.concatenate([acts[2 * pair][...], acts[2 * pair + 1][...]], axis=1)
        taps[pair] = product(fold_ref[...], both)
    for r in range(rows):
        pair, side = r // 2, r % 2
        total = taps[pair, 24 + 24 * side : 48 + 24 * side]
        if side == 0 and pair > 0:
            total = total + taps[pair - 1, 72:96]
        if side == 1 and pair + 1 < half:
            total = total + taps[pair + 1, 0:24]
        both = columns_joined(total)
        for o in range(outs):
            net[o, pl.ds(jnp.where(even, r, rows - 1 - r), 1), :] = both[o : o + 1]
    push = step_factors(index_ref[0])[2]
    for t in range(width // 128):
        at = pl.ds(t * 128, 128)
        for o in range(outs):
            out_ref[o, :, at] = base_ref[o, :, at] + push * net[o, :, at]


def taps_call(first, last, top, bottom, stats, fold, base, index):
    outs, rows, width = base.shape
    chans = top.shape[1]
    return pl.pallas_call(
        taps_kernel,
        out_shape=jax.ShapeDtypeStruct(base.shape, F32),
        in_specs=[VM] * 10 + [SM],
        out_specs=VM,
        scratch_shapes=[pltpu.VMEM((width, chans), BF16)] * (rows - 2)
        + [pltpu.VMEM((rows // 2, 96, width), F32), pltpu.VMEM(base.shape, F32)],
        compiler_params=limit(24),
        cost_estimate=pl.CostEstimate(
            flops=3072 * width * chans * rows, bytes_accessed=1 << 22, transcendentals=1 << 22
        ),
        name="taps",
    )(first, last, top, bottom, *stats, fold, base, index)


def step_kernel(part_ref, core_ref, far_ref, index_ref, next_ref, blocks_ref, kept_ref):
    outs, rows, width = part_ref.shape
    even = (lax.axis_index("tile") & 1) == 0
    push = step_factors(index_ref[0])[2]
    quarter = width // 512
    line = lax.broadcasted_iota(jnp.int32, (rows, 128), 0)
    at_far = line == jnp.where(even, 0, rows - 1)
    at_core = line == jnp.where(even, rows - 1, 0)
    slot = lax.broadcasted_iota(jnp.int32, (rows, 128), 1) // 32
    for t in range(quarter):
        for o in range(outs):
            values = []
            for k in range(4):
                at = pl.ds((quarter * k + t) * 128, 128)
                extra = jnp.where(at_far, far_ref[o : o + 1, at], 0.0)
                extra = jnp.where(at_core, core_ref[o : o + 1, at], extra)
                values.append(part_ref[o, :, at] + push * extra)
                next_ref[o, :, at] = values[-1]
            for j, mixed in enumerate(turn_quarters(values, slot)):
                blocks_ref[4 * t + j, o] = mixed
                kept_ref[4 * t + j, o] = mixed


def step_call(part, core, far, index):
    outs, rows, width = part.shape
    return pl.pallas_call(
        step_kernel,
        out_shape=(
            jax.ShapeDtypeStruct(part.shape, F32),
            jax.ShapeDtypeStruct((width // 128, outs, rows, 128), F32),
            pltpu.VMEM((width // 128, outs, rows, 128), F32),
        ),
        in_specs=[VM] * 3 + [SM],
        out_specs=(VM, VM, VM),
        compiler_params=limit(8),
        name="step",
    )(part, core, far, index)


def sums_kernel(got_ref, reg_ref, out_ref):
    count = got_ref.shape[0]
    shape = got_ref.shape[2:]
    own = lax.broadcasted_iota(jnp.int32, shape, 1) // 32 == lax.axis_index("member") // count
    for o in range(got_ref.shape[1]):
        first = got_ref[0, o]
        second = first * first
        for m in range(1, count):
            value = got_ref[m, o]
            first = first + value
            second = second + value * value
        out_ref[0, o] = first
        out_ref[1, o] = second
        out_ref[2, o] = jnp.where(own, reg_ref[o], 0.0)


def sums_call(got, reg):
    return pl.pallas_call(
        sums_kernel,
        out_shape=jax.ShapeDtypeStruct((3,) + got.shape[1:], F32),
        in_specs=[VM, VM],
        out_specs=VM,
        compiler_params=limit(8),
        name="sums",
    )(got, reg)


STEPS = 32000.0


def coded(values):
    top = jnp.max(jnp.max(jnp.abs(values), axis=1, keepdims=True), axis=0, keepdims=True)
    power = jnp.clip(jnp.ceil(jnp.log2(jnp.maximum(top, 1e-30))), -100.0, 127.0)
    power = jnp.broadcast_to(power, (1, values.shape[1]))
    return jnp.round(values / jnp.exp2(power) * STEPS), power


def as_words(values):
    return values.astype(jnp.int32).astype(jnp.int16)


def as_floats(words):
    return words.astype(jnp.int32).astype(F32)


def spread_kernel(members, one_ref, two_ref, target_ref, out_ref):
    copies, count = out_ref.shape[:2]
    outs = count - 1
    words, powers = [], []
    for o in range(outs):
        mean = (one_ref[0, o] + two_ref[0, o]) / members
        var = (one_ref[1, o] + two_ref[1, o]) / members - mean * mean
        scale = jnp.sqrt(1.0 + target_ref[o] / (var + 1.0))
        offset = one_ref[2, o] + two_ref[2, o] + mean - mean * scale
        high, high_power = coded(scale - 1.0)
        low, low_power = coded(offset)
        words.append(as_words(jnp.concatenate([high, low], axis=0)))
        powers += [high_power, low_power]
    rest = jnp.zeros((16 - len(powers), powers[0].shape[1]), F32)
    words.append(as_words(jnp.concatenate(powers + [rest], axis=0)))
    for k in range(copies):
        for o in range(count):
            out_ref[k, o] = words[o]


def spread_call(one, two, target, copies, members):
    _, outs, rows, lanes = one.shape
    return pl.pallas_call(
        functools.partial(spread_kernel, members),
        out_shape=jax.ShapeDtypeStruct((copies, outs + 1, 2 * rows, lanes), jnp.int16),
        in_specs=[VM, VM, SM],
        out_specs=VM,
        compiler_params=limit(8),
        name="spread",
    )(one, two, target)


def field_kernel(blocks_ref, got_ref, out_ref):
    outs, rows, width = out_ref.shape
    quarter = width // 512
    slot = lax.broadcasted_iota(jnp.int32, (rows, 128), 1) // 32
    for t in range(quarter):
        units = [jnp.exp2(as_floats(got_ref[4 * t + j, outs])) / STEPS for j in range(4)]
        for o in range(outs):
            values = []
            for j in range(4):
                words = as_floats(got_ref[4 * t + j, o])
                scale = 1.0 + words[:rows] * units[j][2 * o : 2 * o + 1]
                offset = words[rows:] * units[j][2 * o + 1 : 2 * o + 2]
                values.append(blocks_ref[4 * t + j, o] * scale + offset)
            for k, mixed in enumerate(turn_quarters(values, slot)):
                out_ref[o, :, pl.ds((quarter * k + t) * 128, 128)] = mixed


def field_call(blocks, got, shape):
    return pl.pallas_call(
        field_kernel,
        out_shape=jax.ShapeDtypeStruct(shape, F32),
        in_specs=[VM, VM],
        out_specs=VM,
        compiler_params=limit(8),
        name="field",
    )(blocks, got)


def swap(value, bits):
    return lax.ppermute(value, "tile", [(i, i ^ bits) for i in range(TILES)])


def far_swap(value):
    return lax.ppermute(value, "tile", [(1, 2), (2, 1)])


def spread_stats(stats):
    return [stats] + [swap(stats, bits) for bits in (1, 2, 3)]


def shards(
    features, residual_state, noise, regression_mean, step_index, conv_first, conv_second, head_weight, spread_target
):
    member = pltpu.with_memory_space_constraint(features[0], pltpu.HBM)
    xt, core, far, stats = features_call(member, 512)
    stats = spread_stats(stats)
    core, far = swap(core, 1), far_swap(far)
    wt, fold, ends = weights_call(conv_first, conv_second, head_weight)
    last, sums, acts = inner_call(xt, core, stats, wt, 1024)
    first, stats = outer_call(acts, far, stats, sums, wt, 1024)
    stats = spread_stats(stats)
    base = base_call(xt, head_weight, residual_state[0], noise[0], step_index)
    core, far, top, bottom = rim_call(first, last, stats, ends)
    core, far = swap(core, 1), far_swap(far)
    part = taps_call(first, last, top, bottom, stats, fold, base, step_index)
    advanced, blocks, kept = step_call(part, core, far, step_index)
    members = lax.axis_size("member")
    size = blocks.shape[0]
    runs = [list(range(i, i + size)) for i in range(0, members, size)]
    got = lax.all_to_all(blocks, "member", 0, 0, tiled=True, axis_index_groups=runs)
    reg = jnp.tile(regression_mean, (1, 1, 4))
    sums = sums_call(got, reg)
    sums = sums + lax.ppermute(sums, "member", [(i, i ^ size) for i in range(members)])
    other = lax.ppermute(sums, "member", [(i, i ^ (3 * size)) for i in range(members)])
    sent = spread_call(sums, other, spread_target, size, members)
    got = lax.all_to_all(sent, "member", 0, 0, tiled=True, axis_index_groups=runs)
    field = field_call(kept, got, advanced.shape)
    return (field[None], advanced[None])


def solution(mesh):
    cells = P("member", None, "tile", None)
    return jax.shard_map(
        shards,
        mesh=mesh,
        in_specs=(cells, cells, cells, P(None, "tile", "member"), P(), P(), P(), P(), P()),
        out_specs=(cells, cells),
        check_vma=False,
    )
```
